256 devices in a mesh: ta: 4 (over y_hi, core), gz: 8 (over z), xy: 8 (over x, y_lo).
Axes of the slice: x: 4, y: 4 (y_hi: 2, y_lo: 2; y = y_hi * 2 + y_lo), z: 8, core: 2. Of those that a mesh axis runs over, the one named last changes fastest.
Arguments:
- fine_source: bfloat16 [4, 32, 8, 8, 2, 2, 2, 1536], P(None, 'ta', 'gz', 'xy'), may hold values from -4 to 4, as said below
- vectors: bfloat16 [32, 8, 8, 2, 2, 2, 32, 1536], P('ta', 'gz', 'xy'), may hold values from -0.75 to 0.75
- coarse_links: bfloat16 [32, 8, 8, 2, 9, 128, 128], P(('ta', 'xy'), 'gz'), may hold values from -1 to 1, as said below
Outputs:
- correction: bfloat16 [4, 32, 8, 8, 2, 2, 2, 1536], P(None, 'ta', 'gz', 'xy')
- coarse_residual: float32 [4, 32, 8, 8, 2, 128], P(None, 'ta', 'gz', 'xy')
The draws below stay inside these ranges and needn't reach their ends.
Inputs may be any that keep to these rules, and one draw needn't show every extreme that they name: `fine_source`: fine residuals of magnitude at most 4. `coarse_links`: operator block entries of magnitude at most 1.
All inputs are finite; a program needn't handle non-finite values.
Results may differ from the reference program's by a relative error of at most 0.011.
Values may be sent and summed in bfloat16 or wider, within the bound.
No kernel may reach another device: no remote copies, remote signals or barrier semaphores. Data moves between devices by JAX's collectives and lax.ppermute only.
A program may use at most 64 MiB of HBM per device.

```python
import jax
import jax.numpy as jnp
from jax import lax

NVEC = 32
FINE = 1536
DOF = 128
RHS = 4
CY = 2
CT = 32
CZ = 8
CX = 8


def position_share(shape):
    time_idx = jax.lax.broadcasted_iota(jnp.float32, shape, 0)
    depth_idx = jax.lax.broadcasted_iota(jnp.float32, shape, 1)
    across_idx = jax.lax.broadcasted_iota(jnp.float32, shape, 2)
    flat = (time_idx * CZ + depth_idx) * CX + across_idx
    return flat / (CT * CZ * CX - 1.0)


def draw_fine_source(key, part):
    key = jax.random.fold_in(key, 11)
    shape = (RHS, CT, CZ, CX, CY, 2, 2, FINE)
    share = position_share((CT, CZ, CX, 1, 1, 1, 1))
    noise = jnp.clip(jax.random.normal(key, shape, jnp.float32), -4.0, 4.0)
    scale = 0.25 * jnp.exp(jnp.log(4.0) * share)
    values = jnp.clip(noise * scale[None], -4.0, 4.0)
    return values.astype(jnp.bfloat16)


def draw_coarse_links(key, part):
    key = jax.random.fold_in(key, 23)
    shape = (CT, CZ, CX, CY, 9, DOF, DOF)
    share = position_share((CT, CZ, CX, 1, 1, 1, 1))
    base = 1.0 / jnp.sqrt(9.0 * DOF)
    noise = jnp.clip(jax.random.normal(key, shape, jnp.float32), -4.0, 4.0)
    scale = 0.5 * jnp.exp(jnp.log(12.0) * share)
    values = jnp.clip(noise * scale * base, -1.0, 1.0)
    return values.astype(jnp.bfloat16)


def levels(key, shape, cuts, low, top_value):
    def one(dim, blocks):
        steps = jax.random.uniform(jax.random.fold_in(jax.random.fold_in(key, 6), dim), (blocks,), jnp.float32, low / len(cuts), top_value / len(cuts))
        return jnp.repeat(jnp.exp(steps), shape[dim] // blocks).reshape((-1,) + (1,) * (len(shape) - dim - 1))

    level = one(*cuts[0])
    for cut in cuts[1:]:
        level = level * one(*cut)
    return level


def scatter_about(rng, shape, deviation, limit, cuts=(), kind=jnp.bfloat16):
    factor_of = levels(rng, shape, cuts, -0.22, 0.18) if cuts else 1.0
    entries = jax.random.normal(rng, shape, jnp.float32) * deviation * factor_of
    return jnp.minimum(jnp.maximum(entries, -limit), limit).astype(kind)


def setup_inputs(seed: int = 0) -> dict:
    seeds = jax.random.split(jax.random.key(seed), 4)
    fine_source = draw_fine_source(jax.random.fold_in(seeds[3], 71), 0)
    vectors = scatter_about(seeds[1], (CT, CZ, CX, CY, 2, 2, NVEC, FINE), (2 * NVEC) ** -0.5, 0.75, ((0, 4), (1, 8), (2, 8)))
    coarse_links = draw_coarse_links(jax.random.fold_in(seeds[3], 71), 0)
    return dict(fine_source=fine_source, vectors=vectors, coarse_links=coarse_links)


def to_slabs(array, lead):
    shaped = array.reshape(array.shape[:lead] + (array.shape[lead] * array.shape[lead + 1],) + array.shape[lead + 2:])
    return jnp.moveaxis(shaped, lead, 0)


def from_slabs(array, lead, times_len, depth_len):
    moved = jnp.moveaxis(array, 0, lead)
    return moved.reshape(moved.shape[:lead] + (times_len, depth_len) + moved.shape[lead + 1:])


def restrict(fine_source, vectors):
    times_len, depth_len = fine_source.shape[1], fine_source.shape[2]

    def one_slab(pieces):
        vector_slab = pieces[0].astype(jnp.float32)
        field_slab = pieces[1].astype(jnp.float32)
        real_part = field_slab[..., 0, :]
        imag_part = field_slab[..., 1, :]
        turned = jnp.stack([imag_part, -real_part], axis=-2)
        stacked = jnp.stack([field_slab, turned], axis=-3)
        coarse = jnp.einsum("xycpki,rxycqpi->rxycqk", vector_slab, stacked)
        return coarse.reshape(coarse.shape[:3] + (-1,))

    result = lax.map(one_slab, (to_slabs(vectors, 0), to_slabs(fine_source, 1)))
    return from_slabs(result, 1, times_len, depth_len)


def prolong(solution, vectors):
    times_len, depth_len = solution.shape[1], solution.shape[2]

    def one_slab(pieces):
        vector_slab = pieces[0].astype(jnp.float32)
        coarse_slab = pieces[1].astype(jnp.float32)
        parts = coarse_slab.reshape(coarse_slab.shape[:3] + (2, 2, -1))
        real_part = parts[..., 0, :]
        imag_part = parts[..., 1, :]
        leading = jnp.stack([real_part, -imag_part], axis=-2)
        trailing = jnp.stack([imag_part, real_part], axis=-2)
        stacked = jnp.stack([leading, trailing], axis=-3)
        fields = jnp.einsum("xycpki,rxycqpk->rxycqi", vector_slab, stacked)
        return fields.astype(jnp.bfloat16)

    result = lax.map(one_slab, (to_slabs(vectors, 0), to_slabs(solution, 1)))
    return from_slabs(result, 1, times_len, depth_len)


def operate(vector, coarse_links):
    rounded = vector.astype(jnp.bfloat16)
    rounded = lax.optimization_barrier(rounded).astype(jnp.float32)
    terms = [rounded]
    for axis in (1, 2, 3, 4):
        terms.append(-jnp.roll(rounded, -1, axis))
        terms.append(-jnp.roll(rounded, 1, axis))
    stacked = jnp.stack(terms, axis=5)
    times_len, depth_len = vector.shape[1], vector.shape[2]

    def one_slab(pieces):
        return jnp.einsum("xydab,rxydb->rxya", pieces[0].astype(jnp.float32), pieces[1])

    hops = lax.map(one_slab, (to_slabs(coarse_links, 0), to_slabs(stacked, 1)))
    return 4.0 * rounded + from_slabs(hops, 1, times_len, depth_len)


def dotted(left, right):
    return jnp.sum(left * right, axis=(1, 2, 3, 4, 5))


def spread(values):
    return values.reshape((-1, 1, 1, 1, 1, 1))


def reference(fine_source, vectors, coarse_links):
    coarse_rhs = restrict(fine_source, vectors)
    image_zero = operate(coarse_rhs, coarse_links)
    norm_zero = dotted(image_zero, image_zero)
    alpha_zero = dotted(image_zero, coarse_rhs) / norm_zero
    iterate_one = spread(alpha_zero) * coarse_rhs
    resid_one = coarse_rhs - spread(alpha_zero) * image_zero
    image_one = operate(resid_one, coarse_links)
    beta_coef = dotted(image_zero, image_one) / norm_zero
    direction = resid_one - spread(beta_coef) * coarse_rhs
    image_one = image_one - spread(beta_coef) * image_zero
    alpha_one = dotted(image_one, resid_one) / dotted(image_one, image_one)
    iterate_two = iterate_one + spread(alpha_one) * direction
    coarse_residual = resid_one - spread(alpha_one) * image_one
    correction = prolong(iterate_two.astype(jnp.bfloat16), vectors)
    return correction, coarse_residual
```

```python
import jax
import jax.numpy as jnp
from jax import lax
from jax.experimental import pallas as pl
from jax.experimental.pallas import tpu as pltpu
from jax.sharding import PartitionSpec as P

F32 = jnp.float32
BF16 = jnp.bfloat16
RHS = 4
ROWS = 8
DOF = 128
VMEM = pl.BlockSpec(memory_space=pltpu.VMEM)


def call(kernel, out_shape, arguments, flops, bytes_accessed):
    return pl.pallas_call(
        kernel,
        out_shape=out_shape,
        in_specs=[VMEM] * len(arguments),
        out_specs=jax.tree.map(lambda _: VMEM, out_shape),
        compiler_params=pltpu.CompilerParams(vmem_limit_bytes=40 * 1024 * 1024),
        cost_estimate=pl.CostEstimate(flops=flops, bytes_accessed=bytes_accessed, transcendentals=0),
    )(*arguments)


def shape(*dims, dtype=F32):
    return jax.ShapeDtypeStruct(dims, dtype)


def index(dims, dim):
    return lax.broadcasted_iota(jnp.int32, dims, dim)


def dot_nt(left, right):
    return lax.dot_general(left, right, (((1,), (1,)), ((), ())), preferred_element_type=F32)


def dot_nn(left, right):
    return lax.dot_general(left, right, (((1,), (0,)), ((), ())), preferred_element_type=F32)


def swap_halves(field):
    return jnp.concatenate([field[4:], field[:4]], axis=0)


def restrict_kernel(source_ref, vectors_ref, out_ref):
    tile = (ROWS, DOF)
    along = index(tile, 0) < RHS
    chirality = index(tile, 1) < 64
    real = (index(tile, 1) // 32) % 2 == 0
    for time in range(source_ref.shape[0]):
        full = dot_nt(source_ref[time], vectors_ref[time])

        def diagonal(part):
            blocks = []
            for c in range(2):
                row = (part * 2 + c) * ROWS
                rows = full[row : row + ROWS]
                blocks.append(jnp.where(along, rows[:, :DOF], rows[:, DOF:]))
            return jnp.where(chirality, blocks[0], blocks[1])

        first, second = diagonal(0), diagonal(1)
        out_ref[time] = jnp.where(
            real, first + pltpu.roll(second, 96, 1), pltpu.roll(second, 32, 1) - first
        )


def split_rows(field):
    high = field.astype(BF16)
    low = (field - high.astype(F32)).astype(BF16)
    return jnp.concatenate([high, low], axis=0)


def blocks_of(links_ref, across, directions):
    return jnp.concatenate(
        [
            jnp.concatenate([links_ref[across, along, d] for d in directions], axis=1)
            for along in range(2)
        ],
        axis=0,
    )


def hop(links_ref, across, fields, directions):
    total = None
    for start in range(0, len(directions), 2):
        rows = jnp.concatenate([split_rows(f) for f in fields[start : start + 2]], axis=1)
        term = dot_nt(rows, blocks_of(links_ref, across, directions[start : start + 2]))
        total = term if total is None else total + term
    along = (index((2 * ROWS, DOF), 0) // RHS) % 2 == 0
    return jnp.where(along, total[:, :DOF], total[:, DOF:])


def center_kernel(field_ref, links_ref, out_ref):
    sites = field_ref.shape[0]
    for across in range(sites):
        own = field_ref[across]
        swapped = -swap_halves(own)
        fields = [
            own,
            -field_ref[(across + 1) % sites],
            -field_ref[(across - 1) % sites],
            swapped,
            swapped,
        ]
        out_ref[across] = hop(links_ref, across, fields, (0, 5, 6, 7, 8))


def image_kernel(center_ref, field_ref, pt_ref, mt_ref, pz_ref, mz_ref, links_ref, image_ref, full_ref):
    for across in range(field_ref.shape[0]):
        fields = [-ref[across] for ref in (pt_ref, mt_ref, pz_ref, mz_ref)]
        hops = center_ref[across] + hop(links_ref, across, fields, (1, 2, 3, 4))
        own = field_ref[across]
        image = 4.0 * own.astype(BF16).astype(F32) + hops[:ROWS]
        image_ref[across] = image
        full_ref[across] = 4.0 * own + hops[:ROWS] + hops[ROWS:]


PAIRS = ((0, 0), (0, 3), (0, 1), (0, 2), (1, 1), (1, 2), (2, 2), (3, 1), (3, 2))


def second_kernel(
    center_ref, image_ref, pt_ref, mt_ref, pz_ref, mz_ref, links_ref, rhs_ref, full_ref, second_ref, sums_ref
):
    totals = [jnp.zeros((ROWS, DOF), F32) for _ in PAIRS]
    for across in range(image_ref.shape[0]):
        fields = [-ref[across] for ref in (pt_ref, mt_ref, pz_ref, mz_ref)]
        hops = center_ref[across] + hop(links_ref, across, fields, (1, 2, 3, 4))
        image = image_ref[across]
        second = 4.0 * image + hops[:ROWS] + hops[ROWS:]
        second_ref[across] = second
        four = (image, full_ref[across], second, rhs_ref[across])
        for number, (left, right) in enumerate(PAIRS):
            totals[number] = totals[number] + four[left] * four[right]
    lane, row = index((ROWS, DOF), 1), index((ROWS, DOF), 0)
    packed = jnp.zeros((ROWS, DOF), F32)
    for number, total in enumerate(totals):
        one = jnp.sum(total, axis=1, keepdims=True)
        packed = packed + jnp.where(lane == number * RHS + row % RHS, one, 0.0)
    packed = jnp.sum(packed, axis=0, keepdims=True)
    sums_ref[...] = jnp.broadcast_to(packed[None], sums_ref.shape)


def pack_kernel(sums_ref, image_ref, full_ref, second_ref, out_ref):
    partial = jnp.sum(sums_ref[...], axis=0)
    partial = jnp.broadcast_to(partial, (ROWS, DOF))
    for across in range(image_ref.shape[0]):
        out_ref[across, 0:8] = image_ref[across]
        out_ref[across, 8:16] = full_ref[across]
        out_ref[across, 16:24] = second_ref[across]
        out_ref[across, 24:32] = partial


def prolong_kernel(packed_ref, rhs_ref, vectors_ref, correction_ref, residual_ref):
    times = packed_ref.shape[0]
    tile = (ROWS, DOF)
    lane, row = index(tile, 1), index(tile, 0)
    total = packed_ref[0, 24:32]
    for time in range(1, times):
        total = total + packed_ref[time, 24:32]
    gram = [
        jnp.sum(jnp.where(lane == number * RHS + row % RHS, total, 0.0), axis=1, keepdims=True)
        for number in range(len(PAIRS))
    ]
    qq, qr, qs, qw, ss, sw, ww, rs, rw = gram
    alpha_zero = qr / qq
    beta = (qs - alpha_zero * qw) / qq
    norm = ss - 2.0 * alpha_zero * sw + alpha_zero * alpha_zero * ww - beta * beta * qq
    alpha_one = (rs - alpha_zero * rw - beta * qr) / norm
    keep_rhs = alpha_zero + alpha_one * (1.0 - beta)
    keep_image = -alpha_one * alpha_zero
    take_image = alpha_zero - alpha_one * beta

    along = row < RHS
    chirality = lane < 64
    real = (lane // 32) % 2 == 0
    spread = (index((32, 32), 1) == (
        (index((32, 32), 0) % 2) * 16
        + ((index((32, 32), 0) // 8) % 2) * 8
        + (index((32, 32), 0) // 16) * 4
        + (index((32, 32), 0) // 2) % 4
    ))
    spread = jnp.where(spread, 1.0, 0.0).astype(BF16)
    for time in range(times):
        rhs = rhs_ref[time]
        image, full, second = (packed_ref[time, i : i + 8] for i in (0, 8, 16))
        residual = rhs - take_image * image - alpha_one * full + (alpha_one * alpha_zero) * second
        for r in range(RHS):
            for y in range(2):
                residual_ref[r, time, 0, 0, y : y + 1] = residual[y * RHS + r : y * RHS + r + 1]
        value = keep_rhs * rhs + keep_image * image
        value = value.astype(BF16).astype(F32)
        firsts = jnp.where(real, value, -value)
        seconds = jnp.where(real, pltpu.roll(value, 96, 1), pltpu.roll(value, 32, 1))
        rows = []
        for part in (firsts, seconds):
            for c in range(2):
                own = jnp.where(chirality == (c == 0), part, 0.0)
                rows.append(jnp.concatenate([jnp.where(along, own, 0.0), jnp.where(along, 0.0, own)], axis=1))
        left = jnp.concatenate(rows, axis=0).astype(BF16)
        left = dot_nn(spread, left).astype(BF16)
        fields = dot_nn(left, vectors_ref[time]).astype(BF16)
        for y in range(2):
            for c in range(2):
                for r in range(RHS):
                    at = ((y * 2 + c) * RHS + r) * 2
                    correction_ref[r, time, 0, 0, y, c] = fields[at : at + 2]


def shifted(array, axis, step):
    devices = lax.axis_size(axis)
    return lax.ppermute(array, axis, [((i + step) % devices, i) for i in range(devices)])


def neighbours(field):
    across_time = ("ta", "xy")
    return (
        shifted(field, across_time, 1),
        shifted(field, across_time, -1),
        shifted(field, "gz", 1),
        shifted(field, "gz", -1),
    )


def exchange(array, axis):
    return lax.all_to_all(array, axis, split_axis=0, concat_axis=0, tiled=True)


def body(fine_source, vectors, coarse_links):
    times = vectors.shape[0]
    sites = coarse_links.shape[2]
    source = fine_source.reshape(RHS, times, 2, 2, 2, -1).transpose(1, 4, 3, 2, 0, 5)
    source = source.reshape(times, 32, -1)
    vectors = vectors.reshape(times, 256, -1)
    links = coarse_links.reshape(coarse_links.shape[2:])
    field = (sites, ROWS, DOF)
    doubled = (sites, 2 * ROWS, DOF)

    fine_rhs = call(
        restrict_kernel, shape(times, ROWS, DOF), (source, vectors), 2 * times * 32 * 256 * 1536, 7_000_000
    )
    rhs = exchange(fine_rhs, "xy")
    around = neighbours(rhs)
    center = call(center_kernel, shape(*doubled), (rhs, links), 2 * sites * 5 * 16 * 256 * 128, 3_000_000)
    image, full = call(
        image_kernel,
        (shape(*field), shape(*field)),
        (center, rhs, *around, links),
        2 * sites * 4 * 16 * 256 * 128,
        2_000_000,
    )
    around = neighbours(image)
    center = call(center_kernel, shape(*doubled), (image, links), 2 * sites * 5 * 16 * 256 * 128, 3_000_000)
    second, sums = call(
        second_kernel,
        (shape(*field), shape(lax.axis_size("ta") * lax.axis_size("gz"), 1, DOF)),
        (center, image, *around, links, rhs, full),
        2 * sites * 4 * 16 * 256 * 128,
        2_000_000,
    )
    sums = exchange(sums, ("ta", "gz"))
    packed = call(pack_kernel, shape(sites, 32, DOF), (sums, image, full, second), 100_000, 200_000)
    packed = exchange(packed, "xy")
    correction, residual = call(
        prolong_kernel,
        (
            shape(RHS, times, 1, 1, 2, 2, 2, vectors.shape[2], dtype=BF16),
            shape(RHS, times, 1, 1, 2, DOF),
        ),
        (packed, fine_rhs, vectors),
        2 * times * 32 * 256 * 1536,
        7_000_000,
    )
    return (correction, residual)


def solution(mesh):
    return jax.shard_map(
        body,
        mesh=mesh,
        in_specs=(
            P(None, "ta", "gz", "xy", None, None, None, None),
            P("ta", "gz", "xy", None, None, None, None, None),
            P(("ta", "xy"), "gz", None, None, None, None, None),
        ),
        out_specs=(
            P(None, "ta", "gz", "xy", None, None, None, None),
            P(None, "ta", "gz", "xy", None, None),
        ),
        check_vma=False,
    )
```

```python
import jax
import jax.numpy as jnp
from jax import lax
from jax.experimental import pallas as pl
from jax.experimental.pallas import tpu as pltpu
from jax.sharding import PartitionSpec as P

F32 = jnp.float32
BF16 = jnp.bfloat16
RHS = 4
LIMIT = 52
ROWS = 8
DOF = 128
VMEM = pl.BlockSpec(memory_space=pltpu.VMEM)


def call(kernel, out_shape, arguments, flops, bytes_accessed, inputs=VMEM, outputs=None, scratch=(), limit=16):
    return pl.pallas_call(
        kernel,
        out_shape=out_shape,
        in_specs=[inputs] * len(arguments),
        out_specs=outputs if outputs is not None else ([VMEM] * len(out_shape) if isinstance(out_shape, tuple) else VMEM),
        scratch_shapes=scratch,
        compiler_params=pltpu.CompilerParams(vmem_limit_bytes=limit * 1024 * 1024),
        cost_estimate=pl.CostEstimate(flops=flops, bytes_accessed=bytes_accessed, transcendentals=0),
    )(*arguments)


def shape(*dims, dtype=F32):
    return pltpu.VMEM(dims, dtype)


def index(dims, dim):
    return lax.broadcasted_iota(jnp.int32, dims, dim)


def dot_nt(left, right):
    return lax.dot_general(left, right, (((1,), (1,)), ((), ())), preferred_element_type=F32)


def dot_nn(left, right):
    return lax.dot_general(left, right, (((1,), (0,)), ((), ())), preferred_element_type=F32)


def swap_halves(field):
    return jnp.concatenate([field[4:], field[:4]], axis=0)


def restrict_kernel(
    source_hbm, vectors_hbm, links_hbm, out_ref, vectors, links, source, rows, full, source_sem, vectors_sem, links_sem
):
    times = vectors.shape[0]
    half = times // 2
    groups = (range(half), range(half, times))
    whole = pltpu.make_async_copy(source_hbm, source, source_sem)
    whole.start()
    copies = []
    for number, group in enumerate(groups):
        span = pl.ds(group[0], len(group))
        copy = pltpu.make_async_copy(vectors_hbm.at[span, 0, 0], vectors.at[span], vectors_sem.at[number])
        copy.start()
        copies.append(copy)
    blocks = pltpu.make_async_copy(links_hbm.at[0, 0], links, links_sem)
    blocks.start()
    tile = (ROWS, DOF)
    along = index(tile, 0) < RHS
    chirality = index(tile, 1) < 64
    real = (index(tile, 1) // 32) % 2 == 0

    def gather(group):
        for time in group:
            for c in range(2):
                for y in range(2):
                    for r in range(RHS):
                        at = ((c * 2 + y) * RHS + r) * 2
                        rows[time, at : at + 2] = source[r, time, 0, 0, y, c]

    def diagonal(time, part):
        one, two = (full[time, y, pl.ds(part, 2 * ROWS, 2), :] for y in range(2))
        picked = [jnp.where(along, one[at : at + ROWS], two[at : at + ROWS]) for at in (0, ROWS)]
        return jnp.where(chirality, picked[0], picked[1])

    def combine(group):
        for time in group:
            first, second = diagonal(time, 0), diagonal(time, 1)
            out_ref[time] = jnp.where(
                real, first + pltpu.roll(second, 96, 1), pltpu.roll(second, 32, 1) - first
            )

    whole.wait()
    gather(groups[0])
    for number, group in enumerate(groups):
        copies[number].wait()
        for time in group:
            product = dot_nt(rows[time], vectors[time].reshape(256, -1))
            full[time, 0], full[time, 1] = product[:, :DOF], product[:, DOF:]
        if number == 0:
            gather(groups[1])
        else:
            combine(groups[0])
    combine(groups[1])
    blocks.wait()


def split_rows(field):
    high = field.astype(BF16)
    low = (field - high.astype(F32)).astype(BF16)
    return jnp.concatenate([high, low], axis=0)


def blocks_of(links_ref, across, directions):
    return jnp.concatenate(
        [
            jnp.concatenate([links_ref[across, along, d] for d in directions], axis=1)
            for along in range(2)
        ],
        axis=0,
    )


def hop(links_ref, across, fields, directions):
    total = None
    for start in range(0, len(directions), 2):
        rows = jnp.concatenate([split_rows(f) for f in fields[start : start + 2]], axis=1)
        term = dot_nt(rows, blocks_of(links_ref, across, directions[start : start + 2]))
        total = term if total is None else total + term
    along = (index((2 * ROWS, DOF), 0) // RHS) % 2 == 0
    return jnp.where(along, total[:, :DOF], total[:, DOF:])


def center_kernel(field_ref, links_ref, out_ref):
    sites = field_ref.shape[0]
    for across in range(sites):
        own = field_ref[across]
        swapped = -swap_halves(own)
        fields = [
            own,
            -field_ref[(across + 1) % sites],
            -field_ref[(across - 1) % sites],
            swapped,
            swapped,
        ]
        out_ref[across] = hop(links_ref, across, fields, (0, 5, 6, 7, 8))


def around_directions():
    time, depth = lax.axis_index("xy") % 2, lax.axis_index("gz") % 2
    return (1 + time, 2 - time, 3 + depth, 4 - depth)


def image_kernel(center_ref, field_ref, t0_ref, t1_ref, z0_ref, z1_ref, links_ref, image_ref, rest_ref):
    directions = around_directions()
    for across in range(field_ref.shape[0]):
        fields = [-ref[across] for ref in (t0_ref, t1_ref, z0_ref, z1_ref)]
        hops = center_ref[across] + hop(links_ref, across, fields, directions)
        own = field_ref[across]
        rounded = own.astype(BF16).astype(F32)
        image_ref[across] = 4.0 * rounded + hops[:ROWS]
        rest_ref[across] = 4.0 * (own - rounded) + hops[ROWS:]


PAIRS = ((0, 0), (0, 1), (2, 2), (2, 3), (3, 3), (0, 2), (0, 3), (2, 1), (3, 1))


def second_kernel(
    center_ref, image_ref, t0_ref, t1_ref, z0_ref, z1_ref, links_ref, rhs_ref, rest_ref, out_ref
):
    directions = around_directions()
    totals = [jnp.zeros((ROWS, DOF), F32) for _ in PAIRS]
    for across in range(image_ref.shape[0]):
        fields = [-ref[across] for ref in (t0_ref, t1_ref, z0_ref, z1_ref)]
        hops = center_ref[across] + hop(links_ref, across, fields, directions)
        hops = hops[:ROWS] + hops[ROWS:]
        image, rest = image_ref[across], rest_ref[across]
        out_ref[across, 0:8] = image
        out_ref[across, 8:16] = rest
        out_ref[across, 16:24] = hops
        four = (image, image - 4.0 * rhs_ref[across], hops, rest)
        for number, (left, right) in enumerate(PAIRS):
            totals[number] = totals[number] + four[left] * four[right]
    lane, row = index((ROWS, DOF), 1), index((ROWS, DOF), 0)
    packed = jnp.zeros((ROWS, DOF), F32)
    for number, total in enumerate(totals):
        one = jnp.sum(total, axis=1, keepdims=True)
        packed = packed + jnp.where(lane == number * RHS + row % RHS, one, 0.0)
    packed = packed + jnp.concatenate([packed[4:], packed[:4]], axis=0)
    for across in range(image_ref.shape[0]):
        out_ref[across, 24:32] = packed


def sums_kernel(packed_ref, out_ref):
    total = packed_ref[0, 24:32]
    for peer in range(1, packed_ref.shape[0]):
        total = total + packed_ref[peer, 24:32]
    total = jnp.where(index((ROWS, DOF), 1) % RHS == index((ROWS, DOF), 0), total, 0.0)
    total = jnp.sum(total, axis=0, keepdims=True)
    out_ref[...] = jnp.broadcast_to(total[None], out_ref.shape)


def block_rows(value):
    tile = (ROWS, DOF)
    along = index(tile, 0) < RHS
    chirality = index(tile, 1) < 64
    real = (index(tile, 1) // 32) % 2 == 0
    firsts = jnp.where(real, value, -value)
    seconds = jnp.where(real, pltpu.roll(value, 96, 1), pltpu.roll(value, 32, 1))
    rows = []
    for part in (firsts, seconds):
        for c in range(2):
            own = jnp.where(chirality == (c == 0), part, 0.0)
            rows.append(jnp.concatenate([jnp.where(along, own, 0.0), jnp.where(along, 0.0, own)], axis=1))
    return jnp.concatenate(rows, axis=0)


def basis_kernel(packed_ref, rhs_ref, vectors_ref, out_ref):
    row, column = index((32, 32), 0), index((32, 32), 1)
    order = column == (row % 2) * 16 + ((row // 8) % 2) * 8 + (row // 16) * 4 + (row // 2) % 4
    order = jnp.where(order, 1.0, 0.0).astype(BF16)
    for time in range(packed_ref.shape[0]):
        parts = []
        for field in (rhs_ref[time], packed_ref[time, 0:8]):
            high = field.astype(BF16).astype(F32)
            for part in (high, field - high):
                parts.append(dot_nn(order, block_rows(part).astype(BF16)).astype(BF16))
        fields = dot_nn(jnp.concatenate(parts, axis=0), vectors_ref[time].reshape(256, -1))
        out_ref[time, 0:32] = fields[0:32] + fields[32:64]
        out_ref[time, 32:64] = fields[64:96] + fields[96:128]


def coefficients(total, numbers):
    lane = index(numbers.shape, 1)
    spread = jnp.broadcast_to(total, numbers.shape)
    gram = [
        jnp.sum(jnp.where(lane == number * RHS + numbers, spread, 0.0), axis=1, keepdims=True)
        for number in range(len(PAIRS))
    ]
    qq, qn, zz, ze, ee, qz, qe, zn, en = gram
    gamma = qn / qq
    alpha_zero = 0.25 * (1.0 - gamma)
    hh = ee - 2.0 * alpha_zero * ze + alpha_zero * alpha_zero * zz
    kappa = (qe - alpha_zero * qz) / qq
    norm = hh - kappa * kappa * qq
    alpha_one = -0.25 * (en - alpha_zero * zn - kappa * qn) / norm
    return alpha_zero, alpha_one, gamma + kappa, kappa


def finish_kernel(sums_ref, packed_ref, rhs_ref, basis_ref, correction_hbm, residual_ref, correction, sems):
    times = packed_ref.shape[0]
    total = jnp.sum(sums_ref[...], axis=0)
    alpha_zero, alpha_one, beta, kappa = coefficients(total, (index((32, DOF), 0) // 2) % RHS)
    keep_rhs = alpha_zero + alpha_one * (1.0 - beta)
    keep_image = -alpha_one * alpha_zero
    copies = []
    for time in range(times):
        fields = (keep_rhs * basis_ref[time, 0:32] + keep_image * basis_ref[time, 32:64]).astype(BF16)
        for y in range(2):
            for c in range(2):
                for r in range(RHS):
                    at = ((y * 2 + c) * RHS + r) * 2
                    correction[r, time, 0, 0, y, c] = fields[at : at + 2]
        copy = pltpu.make_async_copy(correction.at[:, time], correction_hbm.at[:, time], sems.at[time])
        copy.start()
        copies.append(copy)
    alpha_zero, alpha_one, beta, kappa = coefficients(total, index((ROWS, DOF), 0) % RHS)
    for time in range(times):
        image, rest, hops = (packed_ref[time, i : i + 8] for i in (0, 8, 16))
        residual = rhs_ref[time] - (alpha_zero - alpha_one * kappa) * image
        residual = residual - alpha_one * (rest - alpha_zero * hops)
        for r in range(RHS):
            for y in range(2):
                residual_ref[r, time, 0, 0, y : y + 1] = residual[y * RHS + r : y * RHS + r + 1]
    for copy in copies:
        copy.wait()


def neighbours(field):
    found = []
    for axis in (("ta", "xy"), "gz"):
        devices = lax.axis_size(axis)
        for first in range(2):
            pairs = [(i, (i + 1) % devices) for i in range(first, devices, 2)]
            found.append(lax.ppermute(field, axis, pairs + [(j, i) for i, j in pairs]))
    return found


def exchange(array, axis):
    return lax.all_to_all(array, axis, split_axis=0, concat_axis=0, tiled=True)


def body(fine_source, vectors, coarse_links):
    times = vectors.shape[0]
    sites = coarse_links.shape[2]
    field = (sites, ROWS, DOF)
    doubled = (sites, 2 * ROWS, DOF)
    length = vectors.shape[-1]

    anywhere = pl.BlockSpec(memory_space=pl.ANY)
    fine_rhs, vectors, links = call(
        restrict_kernel,
        (
            shape(times, ROWS, DOF),
            shape(*vectors.shape[:1], *vectors.shape[3:], dtype=BF16),
            shape(*coarse_links.shape[2:], dtype=BF16),
        ),
        (fine_source, vectors, coarse_links),
        2 * times * 32 * 256 * length,
        12_000_000,
        inputs=anywhere,
        scratch=[
            pltpu.VMEM(fine_source.shape, BF16),
            pltpu.VMEM((times, 32, length), BF16),
            pltpu.VMEM((times, 2, 32, DOF), F32),
            pltpu.SemaphoreType.DMA,
            pltpu.SemaphoreType.DMA((2,)),
            pltpu.SemaphoreType.DMA,
        ],
        limit=LIMIT,
    )
    rhs = exchange(fine_rhs, "xy")
    around = neighbours(rhs)
    center = call(center_kernel, shape(*doubled), (rhs, links), 2 * sites * 5 * 16 * 256 * 128, 3_000_000)
    image, rest = call(
        image_kernel,
        (shape(*field), shape(*field)),
        (center, rhs, *around, links),
        2 * sites * 4 * 16 * 256 * 128,
        2_000_000,
    )
    around = neighbours(image)
    center = call(center_kernel, shape(*doubled), (image, links), 2 * sites * 5 * 16 * 256 * 128, 3_000_000)
    packed = call(
        second_kernel,
        shape(sites, 32, DOF),
        (center, image, *around, links, rhs, rest),
        2 * sites * 4 * 16 * 256 * 128,
        2_000_000,
    )
    packed = exchange(packed, "xy")
    sums = call(
        sums_kernel, shape(lax.axis_size("ta") * lax.axis_size("gz"), 1, DOF), (packed,), 10_000, 50_000
    )
    sums = exchange(sums, ("ta", "gz"))
    basis = call(
        basis_kernel,
        shape(times, 64, length),
        (packed, fine_rhs, vectors),
        2 * times * 128 * 256 * length,
        10_000_000,
    )
    correction, residual = call(
        finish_kernel,
        (
            jax.ShapeDtypeStruct(fine_source.shape, BF16),
            jax.ShapeDtypeStruct((RHS, times, 1, 1, 2, DOF), F32),
        ),
        (sums, packed, fine_rhs, basis),
        2_000_000,
        4_000_000,
        outputs=(anywhere, VMEM),
        scratch=[pltpu.VMEM(fine_source.shape, BF16), pltpu.SemaphoreType.DMA((times,))],
    )
    return (correction, residual)


def solution(mesh):
    return jax.shard_map(
        body,
        mesh=mesh,
        in_specs=(
            P(None, "ta", "gz", "xy", None, None, None, None),
            P("ta", "gz", "xy", None, None, None, None, None),
            P(("ta", "xy"), "gz", None, None, None, None, None),
        ),
        out_specs=(
            P(None, "ta", "gz", "xy", None, None, None, None),
            P(None, "ta", "gz", "xy", None, None),
        ),
        check_vma=False,
    )
```

```python
import jax
import jax.numpy as jnp
from jax import lax
from jax.experimental import pallas as pl
from jax.experimental.pallas import tpu as pltpu
from jax.sharding import PartitionSpec as P

F32 = jnp.float32
BF16 = jnp.bfloat16
RHS = 4
LIMIT = 56
PARTS = 4
ROWS = 8
DOF = 128
TIME = ("ta", "xy")
EXCHANGES = ((TIME, 0), ("gz", 0), ("gz", 1), (TIME, 1))
VMEM = pl.BlockSpec(memory_space=pltpu.VMEM)


def call(kernel, out_shape, arguments, flops, bytes_accessed, inputs=VMEM, outputs=None, scratch=(), limit=16):
    return pl.pallas_call(
        kernel,
        out_shape=out_shape,
        in_specs=inputs if isinstance(inputs, list) else [inputs] * len(arguments),
        out_specs=outputs if outputs is not None else ([VMEM] * len(out_shape) if isinstance(out_shape, tuple) else VMEM),
        scratch_shapes=scratch,
        compiler_params=pltpu.CompilerParams(vmem_limit_bytes=limit * 1024 * 1024),
        cost_estimate=pl.CostEstimate(flops=flops, bytes_accessed=bytes_accessed, transcendentals=0),
    )(*arguments)


def shape(*dims, dtype=F32):
    return pltpu.VMEM(dims, dtype)


def index(dims, dim):
    return lax.broadcasted_iota(jnp.int32, dims, dim)


def dot_nt(left, right):
    return lax.dot_general(left, right, (((1,), (1,)), ((), ())), preferred_element_type=F32)


def dot_nn(left, right):
    return lax.dot_general(left, right, (((1,), (0,)), ((), ())), preferred_element_type=F32)


def swap_halves(field):
    return jnp.concatenate([field[4:], field[:4]], axis=0)


def restrict_kernel(
    source_hbm, vectors_hbm, links_hbm, out_ref, links, vectors, source, rows, full, source_sem, vectors_sem, links_sem
):
    times = vectors.shape[0]
    half = times // 2
    groups = (range(half), range(half, times))
    whole = pltpu.make_async_copy(source_hbm, source, source_sem)
    whole.start()
    copies = []
    for number, group in enumerate(groups):
        span = pl.ds(group[0], len(group))
        copy = pltpu.make_async_copy(vectors_hbm.at[span, 0, 0], vectors.at[span], vectors_sem.at[number])
        copy.start()
        copies.append(copy)
    blocks = pltpu.make_async_copy(links_hbm.at[0, 0], links, links_sem)
    blocks.start()
    tile = (ROWS, DOF)
    along = index(tile, 0) < RHS
    chirality = index(tile, 1) < 64
    real = (index(tile, 1) // 32) % 2 == 0

    def gather(group):
        for time in group:
            for c in range(2):
                for y in range(2):
                    for r in range(RHS):
                        at = ((c * 2 + y) * RHS + r) * 2
                        rows[time, at : at + 2] = source[r, time, 0, 0, y, c]

    def diagonal(time, part):
        one, two = (full[time, y, pl.ds(part, 2 * ROWS, 2), :] for y in range(2))
        picked = [jnp.where(along, one[at : at + ROWS], two[at : at + ROWS]) for at in (0, ROWS)]
        return jnp.where(chirality, picked[0], picked[1])

    def combine(group):
        for time in group:
            first, second = diagonal(time, 0), diagonal(time, 1)
            out_ref[turned(time, times)] = jnp.where(
                real, first + pltpu.roll(second, 96, 1), pltpu.roll(second, 32, 1) - first
            )

    whole.wait()
    gather(groups[0])
    for number, group in enumerate(groups):
        copies[number].wait()
        for time in group:
            product = dot_nt(rows[time], vectors[time].reshape(256, -1))
            full[time, 0], full[time, 1] = product[:, :DOF], product[:, DOF:]
        if number == 0:
            gather(groups[1])
        else:
            combine(groups[0])
    combine(groups[1])
    blocks.wait()


def split_rows(field):
    high = field.astype(BF16)
    low = (field - high.astype(F32)).astype(BF16)
    return jnp.concatenate([high, low], axis=0)


def blocks_of(links_ref, across, directions):
    return jnp.concatenate(
        [
            jnp.concatenate([links_ref[turned(across), along, d] for d in directions], axis=1)
            for along in range(2)
        ],
        axis=0,
    )


def hop(links_ref, across, fields, directions):
    total = None
    for start in range(0, len(directions), 2):
        rows = jnp.concatenate([split_rows(f) for f in fields[start : start + 2]], axis=1)
        term = dot_nt(rows, blocks_of(links_ref, across, directions[start : start + 2]))
        total = term if total is None else total + term
    along = (index((2 * ROWS, DOF), 0) // RHS) % 2 == 0
    return jnp.where(along, total[:, :DOF], total[:, DOF:])


def center_kernel(field_ref, links_ref, out_ref):
    sites = field_ref.shape[0]
    for across in range(sites):
        own = field_ref[across]
        swapped = -swap_halves(own)
        fields = [
            own,
            -field_ref[(across + 1) % sites],
            -field_ref[(across - 1) % sites],
            swapped,
            swapped,
        ]
        out_ref[across] = hop(links_ref, across, fields, (0, 5, 6, 7, 8))


def around_directions():
    time, depth = lax.axis_index("xy") % 2, lax.axis_index("gz") % 2
    numbers = {("ta", "xy"): (1 + time, 2 - time), "gz": (3 + depth, 4 - depth)}
    return [numbers[axis][first] for axis, first in EXCHANGES]


def image_kernel(center_ref, field_ref, a_ref, b_ref, c_ref, d_ref, links_ref, image_ref, rest_ref):
    directions = around_directions()
    for across in range(field_ref.shape[0]):
        fields = [-ref[across] for ref in (a_ref, b_ref, c_ref, d_ref)]
        hops = center_ref[across] + hop(links_ref, across, fields, directions)
        own = field_ref[across]
        rounded = own.astype(BF16).astype(F32)
        image_ref[across] = 4.0 * rounded + hops[:ROWS]
        rest_ref[across] = 4.0 * (own - rounded) + hops[ROWS:]


PAIRS = ((0, 0), (0, 1), (2, 2), (2, 3), (3, 3), (0, 2), (0, 3), (2, 1), (3, 1))


def second_kernel(
    center_ref, image_ref, a_ref, b_ref, c_ref, d_ref, links_ref, rhs_ref, rest_ref, out_ref
):
    directions = around_directions()
    totals = [jnp.zeros((ROWS, DOF), F32) for _ in PAIRS]
    for across in range(image_ref.shape[0]):
        fields = [-ref[across] for ref in (a_ref, b_ref, c_ref, d_ref)]
        hops = center_ref[across] + hop(links_ref, across, fields, directions)
        hops = hops[:ROWS] + hops[ROWS:]
        image, rest = image_ref[across], rest_ref[across]
        out_ref[across, 0:8] = image
        out_ref[across, 8:16] = rest
        out_ref[across, 16:24] = hops
        four = (image, image - 4.0 * rhs_ref[across], hops, rest)
        for number, (left, right) in enumerate(PAIRS):
            totals[number] = totals[number] + four[left] * four[right]
    lane, row = index((ROWS, DOF), 1), index((ROWS, DOF), 0)
    packed = jnp.zeros((ROWS, DOF), F32)
    for number, total in enumerate(totals):
        one = jnp.sum(total, axis=1, keepdims=True)
        packed = packed + jnp.where(lane == number * RHS + row % RHS, one, 0.0)
    packed = packed + jnp.concatenate([packed[4:], packed[:4]], axis=0)
    for across in range(image_ref.shape[0]):
        out_ref[across, 24:32] = packed


def sums_kernel(packed_ref, out_ref):
    total = packed_ref[0, 24:32]
    for peer in range(1, packed_ref.shape[0]):
        total = total + packed_ref[peer, 24:32]
    total = jnp.where(index((ROWS, DOF), 1) % RHS == index((ROWS, DOF), 0), total, 0.0)
    total = jnp.sum(total, axis=0, keepdims=True)
    out_ref[...] = jnp.broadcast_to(total[None], out_ref.shape)


def block_rows(value):
    tile = (ROWS, DOF)
    along = index(tile, 0) < RHS
    chirality = index(tile, 1) < 64
    real = (index(tile, 1) // 32) % 2 == 0
    firsts = jnp.where(real, value, -value)
    seconds = jnp.where(real, pltpu.roll(value, 96, 1), pltpu.roll(value, 32, 1))
    rows = []
    for part in (firsts, seconds):
        for c in range(2):
            own = jnp.where(chirality == (c == 0), part, 0.0)
            rows.append(jnp.concatenate([jnp.where(along, own, 0.0), jnp.where(along, 0.0, own)], axis=1))
    return jnp.concatenate(rows, axis=0)


def basis_kernel(packed_ref, rhs_ref, vectors_hbm, out_ref, vectors, sems):
    times = vectors.shape[0]
    part = times // PARTS
    copies = []
    for number in range(PARTS):
        span = pl.ds(number * part, part)
        copy = pltpu.make_async_copy(vectors_hbm.at[span, 0, 0], vectors.at[span], sems.at[number])
        copy.start()
        copies.append(copy)
    row, column = index((32, 32), 0), index((32, 32), 1)
    order = column == (row % 2) * 16 + ((row // 8) % 2) * 8 + (row // 16) * 4 + (row // 2) % 4
    order = jnp.where(order, 1.0, 0.0).astype(BF16)
    lefts = []
    for time in range(times):
        pieces = []
        for field in (rhs_ref[turned(time)], packed_ref[turned(time), 0:8]):
            high = field.astype(BF16).astype(F32)
            for piece in (high, field - high):
                pieces.append(dot_nn(order, block_rows(piece).astype(BF16)).astype(BF16))
        lefts.append(jnp.concatenate(pieces, axis=0))
    for time in range(times):
        if time % part == 0:
            copies[time // part].wait()
        fields = dot_nn(lefts[time], vectors[time].reshape(256, -1))
        out_ref[time, 0:32] = fields[0:32] + fields[32:64]
        out_ref[time, 32:64] = fields[64:96] + fields[96:128]


def coefficients(total, numbers):
    lane = index(numbers.shape, 1)
    spread = jnp.broadcast_to(total, numbers.shape)
    gram = [
        jnp.sum(jnp.where(lane == number * RHS + numbers, spread, 0.0), axis=1, keepdims=True)
        for number in range(len(PAIRS))
    ]
    qq, qn, zz, ze, ee, qz, qe, zn, en = gram
    gamma = qn / qq
    alpha_zero = 0.25 * (1.0 - gamma)
    hh = ee - 2.0 * alpha_zero * ze + alpha_zero * alpha_zero * zz
    kappa = (qe - alpha_zero * qz) / qq
    norm = hh - kappa * kappa * qq
    alpha_one = -0.25 * (en - alpha_zero * zn - kappa * qn) / norm
    return alpha_zero, alpha_one, gamma + kappa, kappa


def finish_kernel(
    sums_ref, packed_ref, rhs_ref, basis_ref, correction_hbm, residual_hbm, correction, residual, sems, residual_sem
):
    times = packed_ref.shape[0]
    total = jnp.sum(sums_ref[...], axis=0)
    alpha_zero, alpha_one, beta, kappa = coefficients(total, (index((32, DOF), 0) // 2) % RHS)
    keep_rhs = alpha_zero + alpha_one * (1.0 - beta)
    keep_image = -alpha_one * alpha_zero
    copies = []
    for time in range(times):
        fields = (keep_rhs * basis_ref[time, 0:32] + keep_image * basis_ref[time, 32:64]).astype(BF16)
        for y in range(2):
            for c in range(2):
                for r in range(RHS):
                    at = ((y * 2 + c) * RHS + r) * 2
                    correction[r, time, 0, 0, y, c] = fields[at : at + 2]
        copy = pltpu.make_async_copy(correction.at[:, time], correction_hbm.at[:, time], sems.at[time])
        copy.start()
        copies.append(copy)
        if time == 0:
            alpha_zero, alpha_one, beta, kappa = coefficients(total, index((ROWS, DOF), 0) % RHS)
            for t in range(times):
                image, rest, hops = (packed_ref[turned(t), i : i + 8] for i in (0, 8, 16))
                value = rhs_ref[turned(t)] - (alpha_zero - alpha_one * kappa) * image
                value = value - alpha_one * (rest - alpha_zero * hops)
                for r in range(RHS):
                    for y in range(2):
                        residual[r, t, 0, 0, y : y + 1] = value[y * RHS + r : y * RHS + r + 1]
            copy = pltpu.make_async_copy(residual, residual_hbm, residual_sem)
            copy.start()
            copies.append(copy)
    for copy in copies:
        copy.wait()


def neighbours(field):
    found = []
    for axis, first in EXCHANGES:
        devices = lax.axis_size(axis)
        pairs = [(i, (i + 1) % devices) for i in range(first, devices, 2)]
        found.append(lax.ppermute(field, axis, pairs + [(j, i) for i, j in pairs]))
    return found


def turned(number, devices=8):
    return (number + devices // 2) % devices


def far_first():
    depth = lax.axis_size("gz")
    devices = lax.axis_size("ta") * depth
    return [[(devices // 2 + depth // 2 + i) % devices for i in range(devices)]]


def exchange(array, axis, groups=None):
    return lax.all_to_all(array, axis, split_axis=0, concat_axis=0, tiled=True, axis_index_groups=groups)


def body(fine_source, vectors, coarse_links):
    times = vectors.shape[0]
    sites = coarse_links.shape[2]
    field = (sites, ROWS, DOF)
    doubled = (sites, 2 * ROWS, DOF)
    length = vectors.shape[-1]

    anywhere = pl.BlockSpec(memory_space=pl.ANY)
    local_vectors = pltpu.VMEM(vectors.shape[:1] + vectors.shape[3:], BF16)
    fine_rhs, links = call(
        restrict_kernel,
        (
            shape(times, ROWS, DOF),
            shape(*coarse_links.shape[2:], dtype=BF16),
        ),
        (fine_source, vectors, coarse_links),
        2 * times * 32 * 256 * length,
        12_000_000,
        inputs=anywhere,
        scratch=[
            local_vectors,
            pltpu.VMEM(fine_source.shape, BF16),
            pltpu.VMEM((times, 32, length), BF16),
            pltpu.VMEM((times, 2, 32, DOF), F32),
            pltpu.SemaphoreType.DMA,
            pltpu.SemaphoreType.DMA((2,)),
            pltpu.SemaphoreType.DMA,
        ],
        limit=LIMIT,
    )
    halfway = [[turned(i, sites) for i in range(sites)]]
    rhs = exchange(fine_rhs, "xy", halfway)
    around = neighbours(rhs)
    center = call(center_kernel, shape(*doubled), (rhs, links), 2 * sites * 5 * 16 * 256 * 128, 3_000_000)
    image, rest = call(
        image_kernel,
        (shape(*field), shape(*field)),
        (center, rhs, *around, links),
        2 * sites * 4 * 16 * 256 * 128,
        2_000_000,
    )
    around = neighbours(image)
    center = call(center_kernel, shape(*doubled), (image, links), 2 * sites * 5 * 16 * 256 * 128, 3_000_000)
    packed = call(
        second_kernel,
        shape(sites, 32, DOF),
        (center, image, *around, links, rhs, rest),
        2 * sites * 4 * 16 * 256 * 128,
        2_000_000,
    )
    packed = exchange(packed, "xy", halfway)
    sums = call(
        sums_kernel, shape(lax.axis_size("ta") * lax.axis_size("gz"), 1, DOF), (packed,), 10_000, 50_000
    )
    sums = exchange(sums, ("ta", "gz"), far_first())
    basis = call(
        basis_kernel,
        shape(times, 64, length),
        (packed, fine_rhs, pltpu.with_memory_space_constraint(vectors, pltpu.HBM)),
        2 * times * 128 * 256 * length,
        10_000_000,
        inputs=[VMEM, VMEM, anywhere],
        scratch=[local_vectors, pltpu.SemaphoreType.DMA((PARTS,))],
        limit=24,
    )
    correction, residual = call(
        finish_kernel,
        (
            jax.ShapeDtypeStruct(fine_source.shape, BF16),
            jax.ShapeDtypeStruct((RHS, times, 1, 1, 2, DOF), F32),
        ),
        (sums, packed, fine_rhs, basis),
        2_000_000,
        4_000_000,
        outputs=(anywhere, anywhere),
        scratch=[
            pltpu.VMEM(fine_source.shape, BF16),
            pltpu.VMEM((RHS, times, 1, 1, 2, DOF), F32),
            pltpu.SemaphoreType.DMA((times,)),
            pltpu.SemaphoreType.DMA,
        ],
    )
    return (correction, residual)


def solution(mesh):
    return jax.shard_map(
        body,
        mesh=mesh,
        in_specs=(
            P(None, "ta", "gz", "xy", None, None, None, None),
            P("ta", "gz", "xy", None, None, None, None, None),
            P(("ta", "xy"), "gz", None, None, None, None, None),
        ),
        out_specs=(
            P(None, "ta", "gz", "xy", None, None, None, None),
            P(None, "ta", "gz", "xy", None, None),
        ),
        check_vma=False,
    )
```

```python
import jax
import jax.numpy as jnp
from jax import lax
from jax.experimental import pallas as pl
from jax.experimental.pallas import tpu as pltpu
from jax.sharding import PartitionSpec as P

F32 = jnp.float32
BF16 = jnp.bfloat16
RHS = 4
LIMIT = 56
PARTS = 4
TURN = 4
FIRST = (3, 6)
ROWS = 8
DOF = 128
TIME = ("ta", "xy")
EXCHANGES = ((TIME, 0), ("gz", 0), ("gz", 1), (TIME, 1))
VMEM = pl.BlockSpec(memory_space=pltpu.VMEM)


def call(kernel, out_shape, arguments, flops, bytes_accessed, inputs=VMEM, outputs=None, scratch=(), limit=16):
    return pl.pallas_call(
        kernel,
        out_shape=out_shape,
        in_specs=inputs if isinstance(inputs, list) else [inputs] * len(arguments),
        out_specs=outputs if outputs is not None else ([VMEM] * len(out_shape) if isinstance(out_shape, tuple) else VMEM),
        scratch_shapes=scratch,
        compiler_params=pltpu.CompilerParams(vmem_limit_bytes=limit * 1024 * 1024),
        cost_estimate=pl.CostEstimate(flops=flops, bytes_accessed=bytes_accessed, transcendentals=0),
    )(*arguments)


def shape(*dims, dtype=F32):
    return pltpu.VMEM(dims, dtype)


def index(dims, dim):
    return lax.broadcasted_iota(jnp.int32, dims, dim)


def dot_nt(left, right):
    return lax.dot_general(left, right, (((1,), (1,)), ((), ())), preferred_element_type=F32)


def dot_nn(left, right):
    return lax.dot_general(left, right, (((1,), (0,)), ((), ())), preferred_element_type=F32)


def swap_halves(field):
    return jnp.concatenate([field[4:], field[:4]], axis=0)


def restrict_kernel(
    source_hbm, vectors_hbm, links_hbm, out_ref, links, vectors, source, rows, full, source_sem, vectors_sem, links_sem
):
    times = vectors.shape[0]
    half = times // 2
    groups = (range(half), range(half, times))
    whole = pltpu.make_async_copy(source_hbm, source, source_sem)
    whole.start()
    copies = []
    for number, group in enumerate(groups):
        span = pl.ds(group[0], len(group))
        copy = pltpu.make_async_copy(vectors_hbm.at[span, 0, 0], vectors.at[span], vectors_sem.at[number])
        copy.start()
        copies.append(copy)
    blocks = pltpu.make_async_copy(links_hbm.at[0, 0], links, links_sem)
    blocks.start()
    tile = (ROWS, DOF)
    along = index(tile, 0) < RHS
    chirality = index(tile, 1) < 64
    real = (index(tile, 1) // 32) % 2 == 0

    def gather(group):
        for time in group:
            for c in range(2):
                for y in range(2):
                    for r in range(RHS):
                        at = ((c * 2 + y) * RHS + r) * 2
                        rows[time, at : at + 2] = source[r, time, 0, 0, y, c]

    def diagonal(time, part):
        one, two = (full[time, y, pl.ds(part, 2 * ROWS, 2), :] for y in range(2))
        picked = [jnp.where(along, one[at : at + ROWS], two[at : at + ROWS]) for at in (0, ROWS)]
        return jnp.where(chirality, picked[0], picked[1])

    def combine(group):
        for time in group:
            first, second = diagonal(time, 0), diagonal(time, 1)
            out_ref[place_of(time, times)] = jnp.where(
                real, first + pltpu.roll(second, 96, 1), pltpu.roll(second, 32, 1) - first
            )

    whole.wait()
    gather(groups[0])
    for number, group in enumerate(groups):
        copies[number].wait()
        for time in group:
            product = dot_nt(rows[time], vectors[time].reshape(256, -1))
            full[time, 0], full[time, 1] = product[:, :DOF], product[:, DOF:]
        if number == 0:
            gather(groups[1])
        else:
            combine(groups[0])
    combine(groups[1])
    blocks.wait()


def split_rows(field):
    high = field.astype(BF16)
    low = (field - high.astype(F32)).astype(BF16)
    return jnp.concatenate([high, low], axis=0)


def blocks_of(links_ref, across, directions):
    return jnp.concatenate(
        [
            jnp.concatenate([links_ref[turned(across), along, d] for d in directions], axis=1)
            for along in range(2)
        ],
        axis=0,
    )


def hop(links_ref, across, fields, directions):
    total = None
    for start in range(0, len(directions), 2):
        rows = jnp.concatenate([split_rows(f) for f in fields[start : start + 2]], axis=1)
        term = dot_nt(rows, blocks_of(links_ref, across, directions[start : start + 2]))
        total = term if total is None else total + term
    along = (index((2 * ROWS, DOF), 0) // RHS) % 2 == 0
    return jnp.where(along, total[:, :DOF], total[:, DOF:])


def center_kernel(field_ref, links_ref, out_ref):
    sites = field_ref.shape[0]
    for across in range(sites):
        own = field_ref[across]
        swapped = -swap_halves(own)
        fields = [
            own,
            -field_ref[(across + 1) % sites],
            -field_ref[(across - 1) % sites],
            swapped,
            swapped,
        ]
        out_ref[across] = hop(links_ref, across, fields, (0, 5, 6, 7, 8))


def around_directions():
    time, depth = lax.axis_index("xy") % 2, lax.axis_index("gz") % 2
    numbers = {("ta", "xy"): (1 + time, 2 - time), "gz": (3 + depth, 4 - depth)}
    return [numbers[axis][first] for axis, first in EXCHANGES]


def image_kernel(center_ref, field_ref, a_ref, b_ref, c_ref, d_ref, links_ref, image_ref, rest_ref):
    directions = around_directions()
    for across in range(field_ref.shape[0]):
        fields = [-ref[across] for ref in (a_ref, b_ref, c_ref, d_ref)]
        hops = center_ref[across] + hop(links_ref, across, fields, directions)
        own = field_ref[across]
        rounded = own.astype(BF16).astype(F32)
        image_ref[across] = 4.0 * rounded + hops[:ROWS]
        rest_ref[across] = 4.0 * (own - rounded) + hops[ROWS:]


PAIRS = ((0, 0), (0, 1), (2, 2), (2, 3), (3, 3), (0, 2), (0, 3), (2, 1), (3, 1))


def second_kernel(
    center_ref, image_ref, a_ref, b_ref, c_ref, d_ref, links_ref, rhs_ref, rest_ref, out_ref
):
    directions = around_directions()
    totals = [jnp.zeros((ROWS, DOF), F32) for _ in PAIRS]
    for across in range(image_ref.shape[0]):
        fields = [-ref[across] for ref in (a_ref, b_ref, c_ref, d_ref)]
        hops = center_ref[across] + hop(links_ref, across, fields, directions)
        hops = hops[:ROWS] + hops[ROWS:]
        image, rest = image_ref[across], rest_ref[across]
        out_ref[across, 0:8] = image
        out_ref[across, 8:16] = rest
        out_ref[across, 16:24] = hops
        four = (image, image - 4.0 * rhs_ref[across], hops, rest)
        for number, (left, right) in enumerate(PAIRS):
            totals[number] = totals[number] + four[left] * four[right]
    lane, row = index((ROWS, DOF), 1), index((ROWS, DOF), 0)
    packed = jnp.zeros((ROWS, DOF), F32)
    for number, total in enumerate(totals):
        one = jnp.sum(total, axis=1, keepdims=True)
        packed = packed + jnp.where(lane == number * RHS + row % RHS, one, 0.0)
    packed = packed + jnp.concatenate([packed[4:], packed[:4]], axis=0)
    for across in range(image_ref.shape[0]):
        out_ref[across, 24:32] = packed


def sums_kernel(packed_ref, out_ref):
    total = packed_ref[0, 24:32]
    for peer in range(1, packed_ref.shape[0]):
        total = total + packed_ref[peer, 24:32]
    total = jnp.where(index((ROWS, DOF), 1) % RHS == index((ROWS, DOF), 0), total, 0.0)
    total = jnp.sum(total, axis=0, keepdims=True)
    out_ref[...] = jnp.broadcast_to(total[None], out_ref.shape)


def block_rows(value):
    tile = (ROWS, DOF)
    along = index(tile, 0) < RHS
    chirality = index(tile, 1) < 64
    real = (index(tile, 1) // 32) % 2 == 0
    firsts = jnp.where(real, value, -value)
    seconds = jnp.where(real, pltpu.roll(value, 96, 1), pltpu.roll(value, 32, 1))
    rows = []
    for part in (firsts, seconds):
        for c in range(2):
            own = jnp.where(chirality == (c == 0), part, 0.0)
            rows.append(jnp.concatenate([jnp.where(along, own, 0.0), jnp.where(along, 0.0, own)], axis=1))
    return jnp.concatenate(rows, axis=0)


def basis_kernel(packed_ref, rhs_ref, vectors_hbm, out_ref, vectors, sems):
    times = vectors.shape[0]
    part = times // PARTS
    copies = []
    for number in range(PARTS):
        span = pl.ds(number * part, part)
        copy = pltpu.make_async_copy(vectors_hbm.at[span, 0, 0], vectors.at[span], sems.at[number])
        copy.start()
        copies.append(copy)
    row, column = index((32, 32), 0), index((32, 32), 1)
    order = column == (row % 2) * 16 + ((row // 8) % 2) * 8 + (row // 16) * 4 + (row // 2) % 4
    order = jnp.where(order, 1.0, 0.0).astype(BF16)
    lefts = []
    for time in range(times):
        pieces = []
        for field in (rhs_ref[place_of(time)], packed_ref[place_of(time), 0:8]):
            high = field.astype(BF16).astype(F32)
            for piece in (high, field - high):
                pieces.append(dot_nn(order, block_rows(piece).astype(BF16)).astype(BF16))
        lefts.append(jnp.concatenate(pieces, axis=0))
    for time in range(times):
        if time % part == 0:
            copies[time // part].wait()
        fields = dot_nn(lefts[time], vectors[time].reshape(256, -1))
        out_ref[time, 0:32] = fields[0:32] + fields[32:64]
        out_ref[time, 32:64] = fields[64:96] + fields[96:128]


def coefficients(total, numbers):
    lane = index(numbers.shape, 1)
    spread = jnp.broadcast_to(total, numbers.shape)
    gram = [
        jnp.sum(jnp.where(lane == number * RHS + numbers, spread, 0.0), axis=1, keepdims=True)
        for number in range(len(PAIRS))
    ]
    qq, qn, zz, ze, ee, qz, qe, zn, en = gram
    gamma = qn / qq
    alpha_zero = 0.25 * (1.0 - gamma)
    hh = ee - 2.0 * alpha_zero * ze + alpha_zero * alpha_zero * zz
    kappa = (qe - alpha_zero * qz) / qq
    norm = hh - kappa * kappa * qq
    alpha_one = -0.25 * (en - alpha_zero * zn - kappa * qn) / norm
    return alpha_zero, alpha_one, gamma + kappa, kappa


def finish_kernel(
    sums_ref, packed_ref, rhs_ref, basis_ref, correction_hbm, residual_hbm, correction, residual, sems, residual_sem
):
    times = packed_ref.shape[0]
    total = jnp.sum(sums_ref[...], axis=0)
    alpha_zero, alpha_one, beta, kappa = coefficients(total, (index((32, DOF), 0) // 2) % RHS)
    keep_rhs = alpha_zero + alpha_one * (1.0 - beta)
    keep_image = -alpha_one * alpha_zero
    copies = []
    for time in range(times):
        fields = (keep_rhs * basis_ref[time, 0:32] + keep_image * basis_ref[time, 32:64]).astype(BF16)
        for y in range(2):
            for c in range(2):
                for r in range(RHS):
                    at = ((y * 2 + c) * RHS + r) * 2
                    correction[r, time, 0, 0, y, c] = fields[at : at + 2]
        copy = pltpu.make_async_copy(correction.at[:, time], correction_hbm.at[:, time], sems.at[time])
        copy.start()
        copies.append(copy)
        if time == 0:
            alpha_zero, alpha_one, beta, kappa = coefficients(total, index((ROWS, DOF), 0) % RHS)
            for t in range(times):
                image, rest, hops = (packed_ref[place_of(t), i : i + 8] for i in (0, 8, 16))
                value = rhs_ref[place_of(t)] - (alpha_zero - alpha_one * kappa) * image
                value = value - alpha_one * (rest - alpha_zero * hops)
                for r in range(RHS):
                    for y in range(2):
                        residual[r, t, 0, 0, y : y + 1] = value[y * RHS + r : y * RHS + r + 1]
            copy = pltpu.make_async_copy(residual, residual_hbm, residual_sem)
            copy.start()
            copies.append(copy)
    for copy in copies:
        copy.wait()


def neighbours(field):
    found = []
    for axis, first in EXCHANGES:
        devices = lax.axis_size(axis)
        pairs = [(i, (i + 1) % devices) for i in range(first, devices, 2)]
        found.append(lax.ppermute(field, axis, pairs + [(j, i) for i, j in pairs]))
    return found


def turned(place, devices=8):
    return (place + TURN) % devices


def place_of(number, devices=8):
    return (number - TURN) % devices


def far_first():
    depth = lax.axis_size("gz")
    devices = lax.axis_size("ta") * depth
    return [[(FIRST[0] * depth + FIRST[1] + i) % devices for i in range(devices)]]


def exchange(array, axis, groups=None):
    return lax.all_to_all(array, axis, split_axis=0, concat_axis=0, tiled=True, axis_index_groups=groups)


def body(fine_source, vectors, coarse_links):
    times = vectors.shape[0]
    sites = coarse_links.shape[2]
    field = (sites, ROWS, DOF)
    doubled = (sites, 2 * ROWS, DOF)
    length = vectors.shape[-1]

    anywhere = pl.BlockSpec(memory_space=pl.ANY)
    local_vectors = pltpu.VMEM(vectors.shape[:1] + vectors.shape[3:], BF16)
    fine_rhs, links = call(
        restrict_kernel,
        (
            shape(times, ROWS, DOF),
            shape(*coarse_links.shape[2:], dtype=BF16),
        ),
        (fine_source, vectors, coarse_links),
        2 * times * 32 * 256 * length,
        12_000_000,
        inputs=anywhere,
        scratch=[
            local_vectors,
            pltpu.VMEM(fine_source.shape, BF16),
            pltpu.VMEM((times, 32, length), BF16),
            pltpu.VMEM((times, 2, 32, DOF), F32),
            pltpu.SemaphoreType.DMA,
            pltpu.SemaphoreType.DMA((2,)),
            pltpu.SemaphoreType.DMA,
        ],
        limit=LIMIT,
    )
    halfway = [[turned(i, sites) for i in range(sites)]]
    rhs = exchange(fine_rhs, "xy", halfway)
    around = neighbours(rhs)
    center = call(center_kernel, shape(*doubled), (rhs, links), 2 * sites * 5 * 16 * 256 * 128, 3_000_000)
    image, rest = call(
        image_kernel,
        (shape(*field), shape(*field)),
        (center, rhs, *around, links),
        2 * sites * 4 * 16 * 256 * 128,
        2_000_000,
    )
    around = neighbours(image)
    center = call(center_kernel, shape(*doubled), (image, links), 2 * sites * 5 * 16 * 256 * 128, 3_000_000)
    packed = call(
        second_kernel,
        shape(sites, 32, DOF),
        (center, image, *around, links, rhs, rest),
        2 * sites * 4 * 16 * 256 * 128,
        2_000_000,
    )
    packed = exchange(packed, "xy", halfway)
    sums = call(
        sums_kernel, shape(lax.axis_size("ta") * lax.axis_size("gz"), 1, DOF), (packed,), 10_000, 50_000
    )
    sums = exchange(sums, ("ta", "gz"), far_first())
    basis = call(
        basis_kernel,
        shape(times, 64, length),
        (packed, fine_rhs, pltpu.with_memory_space_constraint(vectors, pltpu.HBM)),
        2 * times * 128 * 256 * length,
        10_000_000,
        inputs=[VMEM, VMEM, anywhere],
        scratch=[local_vectors, pltpu.SemaphoreType.DMA((PARTS,))],
        limit=24,
    )
    correction, residual = call(
        finish_kernel,
        (
            jax.ShapeDtypeStruct(fine_source.shape, BF16),
            jax.ShapeDtypeStruct((RHS, times, 1, 1, 2, DOF), F32),
        ),
        (sums, packed, fine_rhs, basis),
        2_000_000,
        4_000_000,
        outputs=(anywhere, anywhere),
        scratch=[
            pltpu.VMEM(fine_source.shape, BF16),
            pltpu.VMEM((RHS, times, 1, 1, 2, DOF), F32),
            pltpu.SemaphoreType.DMA((times,)),
            pltpu.SemaphoreType.DMA,
        ],
    )
    return (correction, residual)


def solution(mesh):
    return jax.shard_map(
        body,
        mesh=mesh,
        in_specs=(
            P(None, "ta", "gz", "xy", None, None, None, None),
            P("ta", "gz", "xy", None, None, None, None, None),
            P(("ta", "xy"), "gz", None, None, None, None, None),
        ),
        out_specs=(
            P(None, "ta", "gz", "xy", None, None, None, None),
            P(None, "ta", "gz", "xy", None, None),
        ),
        check_vma=False,
    )
```

```python
import jax
import jax.numpy as jnp
from jax import lax
from jax.experimental import pallas as pl
from jax.experimental.pallas import tpu as pltpu
from jax.sharding import PartitionSpec as P

F32 = jnp.float32
BF16 = jnp.bfloat16
RHS = 4
LIMIT = 56
PARTS = 4
TURN = 4
FIRST = (3, 6)
ROWS = 8
DOF = 128
TIME = ("ta", "xy")
EXCHANGES = ((TIME, 0), ("gz", 0), ("gz", 1), (TIME, 1))
VMEM = pl.BlockSpec(memory_space=pltpu.VMEM)


def call(kernel, out_shape, arguments, flops, bytes_accessed, inputs=VMEM, outputs=None, scratch=(), limit=16):
    return pl.pallas_call(
        kernel,
        out_shape=out_shape,
        in_specs=inputs if isinstance(inputs, list) else [inputs] * len(arguments),
        out_specs=outputs if outputs is not None else ([VMEM] * len(out_shape) if isinstance(out_shape, tuple) else VMEM),
        scratch_shapes=scratch,
        compiler_params=pltpu.CompilerParams(vmem_limit_bytes=limit * 1024 * 1024),
        cost_estimate=pl.CostEstimate(flops=flops, bytes_accessed=bytes_accessed, transcendentals=0),
    )(*arguments)


def shape(*dims, dtype=F32):
    return pltpu.VMEM(dims, dtype)


def index(dims, dim):
    return lax.broadcasted_iota(jnp.int32, dims, dim)


def dot_nt(left, right):
    return lax.dot_general(left, right, (((1,), (1,)), ((), ())), preferred_element_type=F32)


def dot_nn(left, right):
    return lax.dot_general(left, right, (((1,), (0,)), ((), ())), preferred_element_type=F32)


def swap_halves(field):
    return jnp.concatenate([field[4:], field[:4]], axis=0)


def restrict_kernel(
    source_hbm, vectors_hbm, links_hbm, out_ref, links, vectors, source, rows, full, source_sem, vectors_sem, links_sem
):
    times = vectors.shape[0]
    half = times // 2
    groups = (range(half), range(half, times))
    whole = pltpu.make_async_copy(source_hbm, source, source_sem)
    whole.start()
    copies = []
    for number, group in enumerate(groups):
        span = pl.ds(group[0], len(group))
        copy = pltpu.make_async_copy(vectors_hbm.at[span, 0, 0], vectors.at[span], vectors_sem.at[number])
        copy.start()
        copies.append(copy)
    blocks = pltpu.make_async_copy(links_hbm.at[0, 0], links, links_sem)
    blocks.start()
    tile = (ROWS, DOF)
    along = index(tile, 0) < RHS
    chirality = index(tile, 1) < 64
    real = (index(tile, 1) // 32) % 2 == 0

    def gather(group):
        for time in group:
            for c in range(2):
                for y in range(2):
                    for r in range(RHS):
                        at = ((c * 2 + y) * RHS + r) * 2
                        rows[time, at : at + 2] = source[r, time, 0, 0, y, c]

    def diagonal(time, part):
        one, two = (full[time, y, pl.ds(part, 2 * ROWS, 2), :] for y in range(2))
        picked = [jnp.where(along, one[at : at + ROWS], two[at : at + ROWS]) for at in (0, ROWS)]
        return jnp.where(chirality, picked[0], picked[1])

    def combine(group):
        for time in group:
            first, second = diagonal(time, 0), diagonal(time, 1)
            out_ref[place_of(time, times)] = jnp.where(
                real, first + pltpu.roll(second, 96, 1), pltpu.roll(second, 32, 1) - first
            )

    whole.wait()
    gather(groups[0])
    for number, group in enumerate(groups):
        copies[number].wait()
        for time in group:
            product = dot_nt(rows[time], vectors[time].reshape(256, -1))
            full[time, 0, 0:32], full[time, 1, 0:32] = product[:, :DOF], product[:, DOF:]
        if number == 0:
            gather(groups[1])
        else:
            combine(groups[0])
    combine(groups[1])
    blocks.wait()


def split_rows(field):
    high = field.astype(BF16)
    low = (field - high.astype(F32)).astype(BF16)
    return jnp.concatenate([high, low], axis=0)


def blocks_of(links_ref, across, directions):
    return jnp.concatenate(
        [
            jnp.concatenate([links_ref[turned(across), along, d] for d in directions], axis=1)
            for along in range(2)
        ],
        axis=0,
    )


def hop(links_ref, across, fields, directions):
    total = None
    for start in range(0, len(directions), 2):
        rows = jnp.concatenate([split_rows(f) for f in fields[start : start + 2]], axis=1)
        term = dot_nt(rows, blocks_of(links_ref, across, directions[start : start + 2]))
        total = term if total is None else total + term
    along = (index((2 * ROWS, DOF), 0) // RHS) % 2 == 0
    return jnp.where(along, total[:, :DOF], total[:, DOF:])


def center_kernel(field_ref, links_ref, out_ref):
    sites = field_ref.shape[0]
    for across in range(sites):
        own = field_ref[across]
        swapped = -swap_halves(own)
        fields = [
            own,
            -field_ref[(across + 1) % sites],
            -field_ref[(across - 1) % sites],
            swapped,
            swapped,
        ]
        out_ref[across] = hop(links_ref, across, fields, (0, 5, 6, 7, 8))


def around_directions():
    time, depth = lax.axis_index("xy") % 2, lax.axis_index("gz") % 2
    numbers = {("ta", "xy"): (1 + time, 2 - time), "gz": (3 + depth, 4 - depth)}
    return [numbers[axis][first] for axis, first in EXCHANGES]


def image_kernel(center_ref, field_ref, a_ref, b_ref, c_ref, d_ref, links_ref, image_ref, rest_ref):
    directions = around_directions()
    for across in range(field_ref.shape[0]):
        fields = [-ref[across] for ref in (a_ref, b_ref, c_ref, d_ref)]
        hops = center_ref[across] + hop(links_ref, across, fields, directions)
        own = field_ref[across]
        rounded = own.astype(BF16).astype(F32)
        image_ref[across] = 4.0 * rounded + hops[:ROWS]
        rest_ref[across] = 4.0 * (own - rounded) + hops[ROWS:]


PAIRS = ((0, 0), (0, 1), (2, 2), (2, 3), (3, 3), (0, 2), (0, 3), (2, 1), (3, 1))


def second_kernel(
    center_ref, image_ref, a_ref, b_ref, c_ref, d_ref, links_ref, rhs_ref, rest_ref, out_ref
):
    directions = around_directions()
    totals = [jnp.zeros((ROWS, DOF), F32) for _ in PAIRS]
    for across in range(image_ref.shape[0]):
        fields = [-ref[across] for ref in (a_ref, b_ref, c_ref, d_ref)]
        hops = center_ref[across] + hop(links_ref, across, fields, directions)
        hops = hops[:ROWS] + hops[ROWS:]
        image, rest = image_ref[across], rest_ref[across]
        out_ref[across, 0:8] = image
        out_ref[across, 8:16] = rest
        out_ref[across, 16:24] = hops
        four = (image, image - 4.0 * rhs_ref[across], hops, rest)
        for number, (left, right) in enumerate(PAIRS):
            totals[number] = totals[number] + four[left] * four[right]
    lane, row = index((ROWS, DOF), 1), index((ROWS, DOF), 0)
    packed = jnp.zeros((ROWS, DOF), F32)
    for number, total in enumerate(totals):
        one = jnp.sum(total, axis=1, keepdims=True)
        packed = packed + jnp.where(lane == number * RHS + row % RHS, one, 0.0)
    packed = packed + jnp.concatenate([packed[4:], packed[:4]], axis=0)
    for across in range(image_ref.shape[0]):
        out_ref[across, 24:32] = packed


def sums_kernel(packed_ref, out_ref):
    total = packed_ref[0, 24:32]
    for peer in range(1, packed_ref.shape[0]):
        total = total + packed_ref[peer, 24:32]
    total = jnp.where(index((ROWS, DOF), 1) % RHS == index((ROWS, DOF), 0), total, 0.0)
    total = jnp.sum(total, axis=0, keepdims=True)
    out_ref[...] = jnp.broadcast_to(total[None], out_ref.shape)


def block_rows(value):
    tile = (ROWS, DOF)
    along = index(tile, 0) < RHS
    chirality = index(tile, 1) < 64
    real = (index(tile, 1) // 32) % 2 == 0
    firsts = jnp.where(real, value, -value)
    seconds = jnp.where(real, pltpu.roll(value, 96, 1), pltpu.roll(value, 32, 1))
    rows = []
    for part in (firsts, seconds):
        for c in range(2):
            own = jnp.where(chirality == (c == 0), part, 0.0)
            rows.append(jnp.concatenate([jnp.where(along, own, 0.0), jnp.where(along, 0.0, own)], axis=1))
    return jnp.concatenate(rows, axis=0)


def basis_kernel(packed_ref, rhs_ref, vectors_hbm, out_ref, vectors, sems):
    times = vectors.shape[0]
    part = times // PARTS
    copies = []
    for number in range(PARTS):
        span = pl.ds(number * part, part)
        copy = pltpu.make_async_copy(vectors_hbm.at[span, 0, 0], vectors.at[span], sems.at[number])
        copy.start()
        copies.append(copy)
    row, column = index((32, 32), 0), index((32, 32), 1)
    order = column == (row % 2) * 16 + ((row // 8) % 2) * 8 + (row // 16) * 4 + (row // 2) % 4
    order = jnp.where(order, 1.0, 0.0).astype(BF16)
    lefts = []
    for time in range(times):
        pieces = []
        for field in (rhs_ref[place_of(time)], packed_ref[place_of(time), 0:8]):
            high = field.astype(BF16).astype(F32)
            for piece in (high, field - high):
                pieces.append(dot_nn(order, block_rows(piece).astype(BF16)).astype(BF16))
        lefts.append(jnp.concatenate(pieces, axis=0))
    for time in range(times):
        if time % part == 0:
            copies[time // part].wait()
        fields = dot_nn(lefts[time], vectors[time].reshape(256, -1))
        out_ref[time, 0:32] = fields[0:32] + fields[32:64]
        out_ref[time, 32:64] = fields[64:96] + fields[96:128]


def coefficients(total, numbers):
    lane = index(numbers.shape, 1)
    spread = jnp.broadcast_to(total, numbers.shape)
    gram = [
        jnp.sum(jnp.where(lane == number * RHS + numbers, spread, 0.0), axis=1, keepdims=True)
        for number in range(len(PAIRS))
    ]
    qq, qn, zz, ze, ee, qz, qe, zn, en = gram
    gamma = qn / qq
    alpha_zero = 0.25 * (1.0 - gamma)
    hh = ee - 2.0 * alpha_zero * ze + alpha_zero * alpha_zero * zz
    kappa = (qe - alpha_zero * qz) / qq
    norm = hh - kappa * kappa * qq
    alpha_one = -0.25 * (en - alpha_zero * zn - kappa * qn) / norm
    return alpha_zero, alpha_one, gamma + kappa, kappa


def finish_kernel(
    sums_ref, packed_ref, rhs_ref, basis_ref, correction_hbm, residual_hbm, correction, residual, sems, residual_sem
):
    times = packed_ref.shape[0]
    total = jnp.sum(sums_ref[...], axis=0)
    alpha_zero, alpha_one, beta, kappa = coefficients(total, (index((32, DOF), 0) // 2) % RHS)
    keep_rhs = alpha_zero + alpha_one * (1.0 - beta)
    keep_image = -alpha_one * alpha_zero
    copies = []
    for time in range(times):
        fields = (keep_rhs * basis_ref[time, 0:32] + keep_image * basis_ref[time, 32:64]).astype(BF16)
        for y in range(2):
            for c in range(2):
                for r in range(RHS):
                    at = ((y * 2 + c) * RHS + r) * 2
                    correction[r, time, 0, 0, y, c] = fields[at : at + 2]
        copy = pltpu.make_async_copy(correction.at[:, time], correction_hbm.at[:, time], sems.at[time])
        copy.start()
        copies.append(copy)
        if time == 0:
            alpha_zero, alpha_one, beta, kappa = coefficients(total, index((ROWS, DOF), 0) % RHS)
            for t in range(times):
                image, rest, hops = (packed_ref[place_of(t), i : i + 8] for i in (0, 8, 16))
                value = rhs_ref[place_of(t)] - (alpha_zero - alpha_one * kappa) * image
                value = value - alpha_one * (rest - alpha_zero * hops)
                for r in range(RHS):
                    for y in range(2):
                        residual[r, t, 0, 0, y : y + 1] = value[y * RHS + r : y * RHS + r + 1]
            copy = pltpu.make_async_copy(residual, residual_hbm, residual_sem)
            copy.start()
            copies.append(copy)
    for copy in copies:
        copy.wait()


def neighbours(field):
    found = []
    for axis, first in EXCHANGES:
        devices = lax.axis_size(axis)
        pairs = [(i, (i + 1) % devices) for i in range(first, devices, 2)]
        found.append(lax.ppermute(field, axis, pairs + [(j, i) for i, j in pairs]))
    return found


def turned(place, devices=8):
    return (place + TURN) % devices


def place_of(number, devices=8):
    return (number - TURN) % devices


def far_first():
    depth = lax.axis_size("gz")
    devices = lax.axis_size("ta") * depth
    return [[(FIRST[0] * depth + FIRST[1] + i) % devices for i in range(devices)]]


def exchange(array, axis, groups=None):
    return lax.all_to_all(array, axis, split_axis=0, concat_axis=0, tiled=True, axis_index_groups=groups)


def body(fine_source, vectors, coarse_links):
    times = vectors.shape[0]
    sites = coarse_links.shape[2]
    field = (sites, ROWS, DOF)
    doubled = (sites, 2 * ROWS, DOF)
    length = vectors.shape[-1]

    anywhere = pl.BlockSpec(memory_space=pl.ANY)
    local_vectors = pltpu.VMEM(vectors.shape[:1] + vectors.shape[3:], BF16)
    fine_rhs, links = call(
        restrict_kernel,
        (
            shape(times, ROWS, DOF),
            shape(*coarse_links.shape[2:], dtype=BF16),
        ),
        (fine_source, vectors, coarse_links),
        2 * times * 32 * 256 * length,
        12_000_000,
        inputs=anywhere,
        scratch=[
            local_vectors,
            pltpu.VMEM(fine_source.shape, BF16),
            pltpu.VMEM((times, 32, length), BF16),
            pltpu.VMEM((times, 2, 40, DOF), F32),
            pltpu.SemaphoreType.DMA,
            pltpu.SemaphoreType.DMA((2,)),
            pltpu.SemaphoreType.DMA,
        ],
        limit=LIMIT,
    )
    halfway = [[turned(i, sites) for i in range(sites)]]
    rhs = exchange(fine_rhs, "xy", halfway)
    around = neighbours(rhs)
    center = call(center_kernel, shape(*doubled), (rhs, links), 2 * sites * 5 * 16 * 256 * 128, 3_000_000)
    image, rest = call(
        image_kernel,
        (shape(*field), shape(*field)),
        (center, rhs, *around, links),
        2 * sites * 4 * 16 * 256 * 128,
        2_000_000,
    )
    around = neighbours(image)
    center = call(center_kernel, shape(*doubled), (image, links), 2 * sites * 5 * 16 * 256 * 128, 3_000_000)
    packed = call(
        second_kernel,
        shape(sites, 32, DOF),
        (center, image, *around, links, rhs, rest),
        2 * sites * 4 * 16 * 256 * 128,
        2_000_000,
    )
    packed = exchange(packed, "xy", halfway)
    sums = call(
        sums_kernel, shape(lax.axis_size("ta") * lax.axis_size("gz"), 1, DOF), (packed,), 10_000, 50_000
    )
    sums = exchange(sums, ("ta", "gz"), far_first())
    basis = call(
        basis_kernel,
        shape(times, 64, length),
        (packed, fine_rhs, pltpu.with_memory_space_constraint(vectors, pltpu.HBM)),
        2 * times * 128 * 256 * length,
        10_000_000,
        inputs=[VMEM, VMEM, anywhere],
        scratch=[local_vectors, pltpu.SemaphoreType.DMA((PARTS,))],
        limit=24,
    )
    correction, residual = call(
        finish_kernel,
        (
            jax.ShapeDtypeStruct(fine_source.shape, BF16),
            jax.ShapeDtypeStruct((RHS, times, 1, 1, 2, DOF), F32),
        ),
        (sums, packed, fine_rhs, basis),
        2_000_000,
        4_000_000,
        outputs=(anywhere, anywhere),
        scratch=[
            pltpu.VMEM(fine_source.shape, BF16),
            pltpu.VMEM((RHS, times, 1, 1, 2, DOF), F32),
            pltpu.SemaphoreType.DMA((times,)),
            pltpu.SemaphoreType.DMA,
        ],
    )
    return (correction, residual)


def solution(mesh):
    return jax.shard_map(
        body,
        mesh=mesh,
        in_specs=(
            P(None, "ta", "gz", "xy", None, None, None, None),
            P("ta", "gz", "xy", None, None, None, None, None),
            P(("ta", "xy"), "gz", None, None, None, None, None),
        ),
        out_specs=(
            P(None, "ta", "gz", "xy", None, None, None, None),
            P(None, "ta", "gz", "xy", None, None),
        ),
        check_vma=False,
    )
```

```python
import jax
import jax.numpy as jnp
from jax import lax
from jax.experimental import pallas as pl
from jax.experimental.pallas import tpu as pltpu
from jax.sharding import PartitionSpec as P

F32 = jnp.float32
BF16 = jnp.bfloat16
RHS = 4
LIMIT = 56
PARTS = 4
TURN = 4
FIRST = (3, 6)
ROWS = 8
DOF = 128
TIME = ("ta", "xy")
EXCHANGES = ((TIME, 0), ("gz", 0), ("gz", 1), (TIME, 1))
VMEM = pl.BlockSpec(memory_space=pltpu.VMEM)


def call(kernel, out_shape, arguments, flops, bytes_accessed, inputs=VMEM, outputs=None, scratch=(), limit=16):
    return pl.pallas_call(
        kernel,
        out_shape=out_shape,
        in_specs=inputs if isinstance(inputs, list) else [inputs] * len(arguments),
        out_specs=outputs if outputs is not None else ([VMEM] * len(out_shape) if isinstance(out_shape, tuple) else VMEM),
        scratch_shapes=scratch,
        compiler_params=pltpu.CompilerParams(vmem_limit_bytes=limit * 1024 * 1024),
        cost_estimate=pl.CostEstimate(flops=flops, bytes_accessed=bytes_accessed, transcendentals=0),
    )(*arguments)


def shape(*dims, dtype=F32):
    return pltpu.VMEM(dims, dtype)


def index(dims, dim):
    return lax.broadcasted_iota(jnp.int32, dims, dim)


def dot_nt(left, right):
    return lax.dot_general(left, right, (((1,), (1,)), ((), ())), preferred_element_type=F32)


def dot_nn(left, right):
    return lax.dot_general(left, right, (((1,), (0,)), ((), ())), preferred_element_type=F32)


def swap_halves(field):
    return jnp.concatenate([field[4:], field[:4]], axis=0)


def restrict_kernel(
    source_hbm, vectors_hbm, links_hbm, out_ref, links, vectors, source, rows, full, source_sem, vectors_sem, links_sem
):
    times = vectors.shape[0]
    half = times // 2
    groups = (range(half), range(half, times))
    whole = pltpu.make_async_copy(source_hbm, source, source_sem)
    whole.start()
    copies = []
    for number, group in enumerate(groups):
        span = pl.ds(group[0], len(group))
        copy = pltpu.make_async_copy(vectors_hbm.at[span, 0, 0], vectors.at[span], vectors_sem.at[number])
        copy.start()
        copies.append(copy)
    blocks = pltpu.make_async_copy(links_hbm.at[0, 0], links, links_sem)
    blocks.start()
    tile = (ROWS, DOF)
    along = index(tile, 0) < RHS
    chirality = index(tile, 1) < 64
    real = (index(tile, 1) // 32) % 2 == 0

    def gather(group):
        for time in group:
            for c in range(2):
                for y in range(2):
                    for r in range(RHS):
                        at = ((c * 2 + y) * RHS + r) * 2
                        rows[time, at : at + 2] = source[r, time, 0, 0, y, c]

    def diagonal(time, part):
        one, two = (full[time, y, pl.ds(part, 2 * ROWS, 2), :] for y in range(2))
        picked = [jnp.where(along, one[at : at + ROWS], two[at : at + ROWS]) for at in (0, ROWS)]
        return jnp.where(chirality, picked[0], picked[1])

    def combine(group):
        for time in group:
            first, second = diagonal(time, 0), diagonal(time, 1)
            out_ref[place_of(time, times)] = jnp.where(
                real, first + pltpu.roll(second, 96, 1), pltpu.roll(second, 32, 1) - first
            )

    whole.wait()
    gather(groups[0])
    for number, group in enumerate(groups):
        copies[number].wait()
        for time in group:
            product = dot_nt(rows[time], vectors[time].reshape(256, -1))
            full[time, 0, 0:32], full[time, 1, 0:32] = product[:, :DOF], product[:, DOF:]
        if number == 0:
            gather(groups[1])
        else:
            combine(groups[0])
    combine(groups[1])
    blocks.wait()


def split_rows(field):
    high = field.astype(BF16)
    low = (field - high.astype(F32)).astype(BF16)
    return jnp.concatenate([high, low], axis=0)


def blocks_of(links_ref, across, directions):
    return jnp.concatenate(
        [
            jnp.concatenate([links_ref[turned(across), along, d] for d in directions], axis=1)
            for along in range(2)
        ],
        axis=0,
    )


def hop(links_ref, across, fields, directions):
    total = None
    for start in range(0, len(directions), 2):
        rows = jnp.concatenate([split_rows(f) for f in fields[start : start + 2]], axis=1)
        term = dot_nt(rows, blocks_of(links_ref, across, directions[start : start + 2]))
        total = term if total is None else total + term
    along = (index((2 * ROWS, DOF), 0) // RHS) % 2 == 0
    return jnp.where(along, total[:, :DOF], total[:, DOF:])


def center_kernel(field_ref, links_ref, out_ref):
    sites = field_ref.shape[0]
    for across in range(sites):
        own = field_ref[across]
        swapped = -swap_halves(own)
        fields = [
            own,
            -field_ref[(across + 1) % sites],
            -field_ref[(across - 1) % sites],
            swapped,
            swapped,
        ]
        out_ref[across] = hop(links_ref, across, fields, (0, 5, 6, 7, 8))


def around_directions():
    time, depth = lax.axis_index("xy") % 2, lax.axis_index("gz") % 2
    numbers = {("ta", "xy"): (1 + time, 2 - time), "gz": (3 + depth, 4 - depth)}
    return [numbers[axis][first] for axis, first in EXCHANGES]


def image_kernel(center_ref, field_ref, a_ref, b_ref, c_ref, d_ref, links_ref, image_ref, rest_ref):
    directions = around_directions()
    for across in range(field_ref.shape[0]):
        fields = [-ref[across] for ref in (a_ref, b_ref, c_ref, d_ref)]
        hops = center_ref[across] + hop(links_ref, across, fields, directions)
        own = field_ref[across]
        rounded = own.astype(BF16).astype(F32)
        image_ref[across] = 4.0 * rounded + hops[:ROWS]
        rest_ref[across] = 4.0 * (own - rounded) + hops[ROWS:]


PAIRS = ((0, 0), (0, 1), (2, 2), (2, 3), (3, 3), (0, 2), (0, 3), (2, 1), (3, 1))


def second_kernel(
    center_ref, image_ref, a_ref, b_ref, c_ref, d_ref, links_ref, rhs_ref, rest_ref, out_ref
):
    directions = around_directions()
    totals = [jnp.zeros((ROWS, DOF), F32) for _ in PAIRS]
    for across in range(image_ref.shape[0]):
        fields = [-ref[across] for ref in (a_ref, b_ref, c_ref, d_ref)]
        hops = center_ref[across] + hop(links_ref, across, fields, directions)
        hops = hops[:ROWS] + hops[ROWS:]
        image, rest = image_ref[across], rest_ref[across]
        out_ref[across, 0:8] = image
        out_ref[across, 8:16] = rest
        out_ref[across, 16:24] = hops
        four = (image, image - 4.0 * rhs_ref[across], hops, rest)
        for number, (left, right) in enumerate(PAIRS):
            totals[number] = totals[number] + four[left] * four[right]
    lane, row = index((ROWS, DOF), 1), index((ROWS, DOF), 0)
    packed = jnp.zeros((ROWS, DOF), F32)
    for number, total in enumerate(totals):
        one = jnp.sum(total, axis=1, keepdims=True)
        packed = packed + jnp.where(lane == number * RHS + row % RHS, one, 0.0)
    packed = packed + jnp.concatenate([packed[4:], packed[:4]], axis=0)
    for across in range(image_ref.shape[0]):
        out_ref[across, 24:32] = packed


def sums_kernel(packed_ref, out_ref):
    total = packed_ref[0, 24:32]
    for peer in range(1, packed_ref.shape[0]):
        total = total + packed_ref[peer, 24:32]
    total = jnp.where(index((ROWS, DOF), 1) % RHS == index((ROWS, DOF), 0), total, 0.0)
    total = jnp.sum(total, axis=0, keepdims=True)
    out_ref[...] = jnp.broadcast_to(total[None], out_ref.shape)


def block_rows(value):
    tile = (ROWS, DOF)
    along = index(tile, 0) < RHS
    chirality = index(tile, 1) < 64
    real = (index(tile, 1) // 32) % 2 == 0
    firsts = jnp.where(real, value, -value)
    seconds = jnp.where(real, pltpu.roll(value, 96, 1), pltpu.roll(value, 32, 1))
    rows = []
    for part in (firsts, seconds):
        for c in range(2):
            own = jnp.where(chirality == (c == 0), part, 0.0)
            rows.append(jnp.concatenate([jnp.where(along, own, 0.0), jnp.where(along, 0.0, own)], axis=1))
    return jnp.concatenate(rows, axis=0)


def basis_kernel(packed_ref, rhs_ref, vectors_hbm, out_ref, vectors, sems):
    times = vectors.shape[0]
    part = times // PARTS
    copies = []
    for number in range(PARTS):
        span = pl.ds(number * part, part)
        copy = pltpu.make_async_copy(vectors_hbm.at[span, 0, 0], vectors.at[span], sems.at[number])
        copy.start()
        copies.append(copy)
    row, column = index((32, 32), 0), index((32, 32), 1)
    order = column == (row % 2) * 16 + ((row // 8) % 2) * 8 + (row // 16) * 4 + (row // 2) % 4
    order = jnp.where(order, 1.0, 0.0).astype(BF16)
    lefts = []
    for time in range(times):
        pieces = []
        for field in (rhs_ref[place_of(time)], packed_ref[place_of(time), 0:8]):
            high = field.astype(BF16).astype(F32)
            for piece in (high, field - high):
                pieces.append(dot_nn(order, block_rows(piece).astype(BF16)).astype(BF16))
        lefts.append(jnp.concatenate(pieces, axis=0))
    for time in range(times):
        if time % part == 0:
            copies[time // part].wait()
        fields = dot_nn(lefts[time], vectors[time].reshape(256, -1))
        out_ref[time, 0:32] = fields[0:32] + fields[32:64]
        out_ref[time, 32:64] = fields[64:96] + fields[96:128]


def coefficients(total, numbers):
    lane = index(numbers.shape, 1)
    spread = jnp.broadcast_to(total, numbers.shape)
    gram = [
        jnp.sum(jnp.where(lane == number * RHS + numbers, spread, 0.0), axis=1, keepdims=True)
        for number in range(len(PAIRS))
    ]
    qq, qn, zz, ze, ee, qz, qe, zn, en = gram
    gamma = qn / qq
    alpha_zero = 0.25 * (1.0 - gamma)
    hh = ee - 2.0 * alpha_zero * ze + alpha_zero * alpha_zero * zz
    kappa = (qe - alpha_zero * qz) / qq
    norm = hh - kappa * kappa * qq
    alpha_one = -0.25 * (en - alpha_zero * zn - kappa * qn) / norm
    return alpha_zero, alpha_one, gamma + kappa, kappa


def finish_kernel(
    sums_ref, packed_ref, rhs_ref, basis_ref, correction_hbm, residual_hbm, correction, residual, sems, residual_sem
):
    times = packed_ref.shape[0]
    total = jnp.sum(sums_ref[...], axis=0)
    alpha_zero, alpha_one, beta, kappa = coefficients(total, (index((ROWS, DOF), 0) // 2) % RHS)
    keep_rhs = jnp.concatenate([alpha_zero + alpha_one * (1.0 - beta)] * 4, axis=0)
    keep_image = jnp.concatenate([-alpha_one * alpha_zero] * 4, axis=0)
    copies = []
    for time in range(times):
        fields = (keep_rhs * basis_ref[time, 0:32] + keep_image * basis_ref[time, 32:64]).astype(BF16)
        for y in range(2):
            for c in range(2):
                for r in range(RHS):
                    at = ((y * 2 + c) * RHS + r) * 2
                    correction[r, time, 0, 0, y, c] = fields[at : at + 2]
        copy = pltpu.make_async_copy(correction.at[:, time], correction_hbm.at[:, time], sems.at[time])
        copy.start()
        copies.append(copy)
        if time == 0:
            alpha_zero, alpha_one, beta, kappa = coefficients(total, index((ROWS, DOF), 0) % RHS)
            for t in range(times):
                image, rest, hops = (packed_ref[place_of(t), i : i + 8] for i in (0, 8, 16))
                value = rhs_ref[place_of(t)] - (alpha_zero - alpha_one * kappa) * image
                value = value - alpha_one * (rest - alpha_zero * hops)
                for r in range(RHS):
                    for y in range(2):
                        residual[r, t, 0, 0, y : y + 1] = value[y * RHS + r : y * RHS + r + 1]
            copy = pltpu.make_async_copy(residual, residual_hbm, residual_sem)
            copy.start()
            copies.append(copy)
    for copy in copies:
        copy.wait()


def neighbours(field):
    found = []
    for axis, first in EXCHANGES:
        devices = lax.axis_size(axis)
        pairs = [(i, (i + 1) % devices) for i in range(first, devices, 2)]
        found.append(lax.ppermute(field, axis, pairs + [(j, i) for i, j in pairs]))
    return found


def turned(place, devices=8):
    return (place + TURN) % devices


def place_of(number, devices=8):
    return (number - TURN) % devices


def far_first():
    depth = lax.axis_size("gz")
    devices = lax.axis_size("ta") * depth
    return [[(FIRST[0] * depth + FIRST[1] + i) % devices for i in range(devices)]]


def exchange(array, axis, groups=None):
    return lax.all_to_all(array, axis, split_axis=0, concat_axis=0, tiled=True, axis_index_groups=groups)


def body(fine_source, vectors, coarse_links):
    times = vectors.shape[0]
    sites = coarse_links.shape[2]
    field = (sites, ROWS, DOF)
    doubled = (sites, 2 * ROWS, DOF)
    length = vectors.shape[-1]

    anywhere = pl.BlockSpec(memory_space=pl.ANY)
    local_vectors = pltpu.VMEM(vectors.shape[:1] + vectors.shape[3:], BF16)
    fine_rhs, links = call(
        restrict_kernel,
        (
            shape(times, ROWS, DOF),
            shape(*coarse_links.shape[2:], dtype=BF16),
        ),
        (fine_source, vectors, coarse_links),
        2 * times * 32 * 256 * length,
        12_000_000,
        inputs=anywhere,
        scratch=[
            local_vectors,
            pltpu.VMEM(fine_source.shape, BF16),
            pltpu.VMEM((times, 32, length), BF16),
            pltpu.VMEM((times, 2, 40, DOF), F32),
            pltpu.SemaphoreType.DMA,
            pltpu.SemaphoreType.DMA((2,)),
            pltpu.SemaphoreType.DMA,
        ],
        limit=LIMIT,
    )
    halfway = [[turned(i, sites) for i in range(sites)]]
    rhs = exchange(fine_rhs, "xy", halfway)
    around = neighbours(rhs)
    center = call(center_kernel, shape(*doubled), (rhs, links), 2 * sites * 5 * 16 * 256 * 128, 3_000_000)
    image, rest = call(
        image_kernel,
        (shape(*field), shape(*field)),
        (center, rhs, *around, links),
        2 * sites * 4 * 16 * 256 * 128,
        2_000_000,
    )
    around = neighbours(image)
    center = call(center_kernel, shape(*doubled), (image, links), 2 * sites * 5 * 16 * 256 * 128, 3_000_000)
    packed = call(
        second_kernel,
        shape(sites, 32, DOF),
        (center, image, *around, links, rhs, rest),
        2 * sites * 4 * 16 * 256 * 128,
        2_000_000,
    )
    packed = exchange(packed, "xy", halfway)
    sums = call(
        sums_kernel, shape(lax.axis_size("ta") * lax.axis_size("gz"), 1, DOF), (packed,), 10_000, 50_000
    )
    sums = exchange(sums, ("ta", "gz"), far_first())
    basis = call(
        basis_kernel,
        shape(times, 64, length),
        (packed, fine_rhs, pltpu.with_memory_space_constraint(vectors, pltpu.HBM)),
        2 * times * 128 * 256 * length,
        10_000_000,
        inputs=[VMEM, VMEM, anywhere],
        scratch=[local_vectors, pltpu.SemaphoreType.DMA((PARTS,))],
        limit=24,
    )
    correction, residual = call(
        finish_kernel,
        (
            jax.ShapeDtypeStruct(fine_source.shape, BF16),
            jax.ShapeDtypeStruct((RHS, times, 1, 1, 2, DOF), F32),
        ),
        (sums, packed, fine_rhs, basis),
        2_000_000,
        4_000_000,
        outputs=(anywhere, anywhere),
        scratch=[
            pltpu.VMEM(fine_source.shape, BF16),
            pltpu.VMEM((RHS, times, 1, 1, 2, DOF), F32),
            pltpu.SemaphoreType.DMA((times,)),
            pltpu.SemaphoreType.DMA,
        ],
    )
    return (correction, residual)


def solution(mesh):
    return jax.shard_map(
        body,
        mesh=mesh,
        in_specs=(
            P(None, "ta", "gz", "xy", None, None, None, None),
            P("ta", "gz", "xy", None, None, None, None, None),
            P(("ta", "xy"), "gz", None, None, None, None, None),
        ),
        out_specs=(
            P(None, "ta", "gz", "xy", None, None, None, None),
            P(None, "ta", "gz", "xy", None, None),
        ),
        check_vma=False,
    )
```
